128 devices in a mesh: contrast: 4 (over x), pa: 2 (over core), pb: 16 (over z, y).
Axes of the slice: x: 4, y: 4, z: 4, core: 2. Of those that a mesh axis runs over, the one named last changes fastest.
Arguments:
- image: float32 [4, 2, 128, 160, 128], P('contrast', None, 'pa', 'pb'), may hold values from -9 to 9
- coil_maps: bfloat16 [4, 2, 128, 160, 128], P(None, None, 'pa', 'pb'), may hold values from -2 to 2
- kspace: bfloat16 [4, 4, 2, 128, 160, 128], P('contrast', None, None, ('pa', 'pb')), may hold values from -4 to 4
- sampling: int32 [4, 128, 160, 128], P('contrast', ('pa', 'pb')), may hold values 0 or 1
- available: int32 [4], P('contrast'), may hold values from 0 to 1, as said below
Outputs:
- image_next: float32 [4, 2, 128, 160, 128], P('contrast', None, 'pa', 'pb')
- misfit: float32 [], replicated
The draws below stay inside these ranges and needn't reach their ends.
Inputs may be any that keep to these rules, and one draw needn't show every extreme that they name: `available`: at least one contrast is missing, and at most max(1, 1) are.
All inputs are finite; a program needn't handle non-finite values. No bound on the sum of `sampling` on one device may be relied on, other than what follows from the above.
Results may differ from the reference program's by a relative error of at most 0.0003.
Values sent between devices are 32-bit elements; how exact they have to be, the bound alone decides.
No kernel may reach another device: no remote copies, remote signals or barrier semaphores. Data moves between devices by JAX's collectives and lax.ppermute only.
A program may use at most 64 MiB of HBM per device.

```python
import jax
import jax.numpy as jnp
from jax import lax

NX = 128
NY = 160
NZ = 128
COILS = 4
CON = 4


def draw_image(key, part):
    base_key = jax.random.fold_in(key, 0)
    extent = (CON, 2, NX, NY, NZ)
    strength = 0.5 + jnp.arange(CON, dtype=jnp.float32) / max(CON - 1, 1)
    strength = strength.reshape(CON, 1, 1, 1, 1)
    sample = jnp.clip(jax.random.normal(base_key, extent, jnp.float32), -4.0, 4.0)
    return sample * strength


def draw_kspace(key, part):
    extent = (CON, COILS, 2, NZ, NY, NX)
    envelope = 0.3 * (1.0 + 2.0 * jnp.arange(NZ, dtype=jnp.float32) / max(NZ - 1, 1))
    envelope = envelope.reshape(1, 1, 1, NZ, 1, 1)
    sample = jnp.clip(jax.random.normal(key, extent, jnp.float32), -4.0, 4.0)
    return (sample * envelope).astype(jnp.bfloat16)


def draw_available(key, part):
    order_key, count_key = jax.random.split(key)
    ordering = jax.random.permutation(order_key, CON)
    missing = jax.random.randint(count_key, (), 1, max(1, CON // 4) + 1)
    return (ordering >= missing).astype(jnp.int32)


def touch_ends(entries, key, least, high):
    longest = entries.shape.index(max(entries.shape))
    spots = []
    for shift in (0, 1):
        where = [jax.random.randint(jax.random.fold_in(key, axis), (), 0, length) for axis, length in enumerate(entries.shape)]
        where[longest] = (where[longest] + shift) % entries.shape[longest]
        spots.append(tuple(where))
    return entries.at[spots[0]].set(least).at[spots[1]].set(high)


def block_levels(stream_key, shape, cuts, smallest, top_value):
    def one(axis_at, parts):
        draws = jax.random.uniform(jax.random.fold_in(jax.random.fold_in(stream_key, 6), axis_at), (parts,), jnp.float32, smallest / len(cuts), top_value / len(cuts))
        return jnp.repeat(jnp.exp(draws), shape[axis_at] // parts).reshape((-1,) + (1,) * (len(shape) - axis_at - 1))

    factor_of = one(*cuts[0])
    for cut in cuts[1:]:
        factor_of = factor_of * one(*cut)
    return factor_of


def gaussian(key, dims, spread, limit, shards=(), kind=jnp.bfloat16):
    array = spread * jax.random.normal(key, dims, jnp.float32)
    if shards:
        array = array * block_levels(key, dims, shards, -0.22, 0.18)
    return jnp.clip(array, -limit, limit).astype(kind)


def setup_inputs(seed: int = 0) -> dict:
    seeds = jax.random.split(jax.random.key(seed), 6)
    image = draw_image(jax.random.fold_in(seeds[5], 71), 0)
    coil_maps = gaussian(seeds[1], (COILS, 2, NX, NY, NZ), (0.7 / COILS ** 0.5), 2.0, ((2, 2), (3, 16)))
    kspace = draw_kspace(jax.random.fold_in(seeds[5], 71), 0)
    sampling = touch_ends((jax.random.randint(seeds[3], (CON, NZ, NY, NX), 0, 3) < 1).astype(jnp.int32), jax.random.fold_in(seeds[3], 1), 0, 1)
    available = draw_available(jax.random.fold_in(seeds[5], 71), 0)
    return dict(image=image, coil_maps=coil_maps, kspace=kspace, sampling=sampling, available=available)


step_size = 1.0
threshold = 2.5

def reference(image, coil_maps, kspace, sampling, available):
    sensitivity = coil_maps[:, 0].astype(jnp.float32) + 1j * coil_maps[:, 1].astype(jnp.float32)

    def per_contrast(entry):
        pixels, measured, mask_rows, present_flag = entry
        weight_factor = mask_rows.astype(jnp.float32) * present_flag.astype(jnp.float32)
        complex_image = pixels[0] + 1j * pixels[1]

        def per_coil(running, coil_element):
            single_sensitivity, single_measurement = coil_element
            fourier_coefficients = jnp.transpose(jnp.fft.fftn(single_sensitivity * complex_image, norm='ortho'), (2, 1, 0))
            measurement_value = single_measurement[0].astype(jnp.float32) + 1j * single_measurement[1].astype(jnp.float32)
            kspace_residual = weight_factor * (fourier_coefficients - measurement_value)
            returned = jnp.fft.ifftn(jnp.transpose(kspace_residual, (2, 1, 0)), norm='ortho')
            combined = jnp.conj(single_sensitivity) * returned
            grad_re = running[0] + jnp.real(combined).astype(jnp.float32)
            grad_im = running[1] + jnp.imag(combined).astype(jnp.float32)
            res_re = jnp.real(kspace_residual)
            res_im = jnp.imag(kspace_residual)
            misfit = running[2] + jnp.sum(res_re * res_re + res_im * res_im).astype(jnp.float32)
            return ((grad_re, grad_im, misfit), None)
        initial = (jnp.zeros(pixels.shape[1:], jnp.float32), jnp.zeros(pixels.shape[1:], jnp.float32), jnp.zeros((), jnp.float32))
        totals, _ = lax.scan(per_coil, initial, (sensitivity, measured))
        return totals
    grad_re, grad_im, misfits = lax.map(per_contrast, (image, kspace, sampling, available))
    present = available.astype(jnp.float32)[:, None, None, None]
    moved_re = image[:, 0] - step_size * grad_re
    moved_im = image[:, 1] - step_size * grad_im
    energy = present * (moved_re * moved_re + moved_im * moved_im)
    norm_value = jnp.sqrt(lax.optimization_barrier(jnp.sum(energy, axis=0)))
    factor = jnp.maximum(norm_value - threshold, 0.0) / jnp.maximum(norm_value, threshold)
    shrink = present * factor[None]
    image_next = jnp.stack([moved_re * shrink, moved_im * shrink], axis=1)
    misfit = jnp.sum(misfits) / (2.0 * CON * COILS * NX * NY * NZ)
    return (image_next, misfit)
```

```python
import functools
import math

import jax
import jax.numpy as jnp
import ml_dtypes
import numpy as np
from jax import lax
from jax.experimental import pallas as pl
from jax.experimental.pallas import tpu as pltpu
from jax.sharding import PartitionSpec as P

step_size = 1.0
threshold = 2.5
LANES = 128
VMEM_LIMIT = 40 * 1024 * 1024


def trig(length):
    index = np.arange(length)
    angles = (index[:, None] * index[None, :] % length) * (2.0 * math.pi / length)
    scale = 1.0 / math.sqrt(length)
    return np.cos(angles) * scale, np.sin(angles) * scale


def halves(table):
    high = table.astype(np.float32).astype(ml_dtypes.bfloat16)
    low = (table - high.astype(np.float64)).astype(np.float32).astype(ml_dtypes.bfloat16)
    return high, low


def left_table(table):
    high, low = halves(table)
    return np.concatenate([high, high, low], axis=1)


def right_table(table):
    high, low = halves(table)
    return np.concatenate([high, high, low], axis=0)


def split_data(value, axis):
    high = value.astype(jnp.bfloat16)
    low = (value - high.astype(jnp.float32)).astype(jnp.bfloat16)
    return jnp.concatenate([high, low, high], axis=axis)


def dot(left, right, dims):
    return lax.dot_general(left, right, (dims, ((), ())), preferred_element_type=jnp.float32)


def z_forward_table(depth):
    c, s = trig(depth)
    re_row = np.concatenate([c, s], axis=1)
    im_row = np.concatenate([-s, c], axis=1)
    return left_table(np.stack([re_row, im_row], axis=1).reshape(2 * depth, 2 * depth))


def z_inverse_table(depth):
    c, s = trig(depth)
    re_row = np.concatenate([c, s], axis=1)
    im_row = np.concatenate([-s, c], axis=1)
    return right_table(np.stack([re_row, im_row], axis=1).reshape(2 * depth, 2 * depth))


def x_table(width, sign):
    c, s = trig(width)
    s = sign * s
    return right_table(np.concatenate([np.concatenate([c, s], 1), np.concatenate([-s, c], 1)], 0))


def y_order(groups, rows):
    y = np.arange(groups * rows).reshape(groups, rows // 2, 2)
    return y.transpose(2, 0, 1).reshape(-1)


def y_forward_table(width, order):
    c, s = trig(width)
    return left_table(np.concatenate([c[:, order], s[:, order]], axis=0))


def y_inverse_table(width, order):
    c, s = trig(width)
    return left_table(np.concatenate([c[order], s[order]], axis=0))


def z_forward_kernel(image_ref, maps_ref, table_ref, out_ref):
    rows = image_ref.shape[1] * image_ref.shape[2]
    depth = image_ref.shape[3]
    image_re = image_ref[0].reshape(rows, depth)
    image_im = image_ref[1].reshape(rows, depth)
    maps_re = maps_ref[0, 0].reshape(rows, depth).astype(jnp.float32)
    maps_im = maps_ref[0, 1].reshape(rows, depth).astype(jnp.float32)
    product = jnp.concatenate(
        [maps_re * image_re - maps_im * image_im, maps_re * image_im + maps_im * image_re], axis=1
    )
    result = dot(table_ref[...], split_data(product, 1), ((1,), (1,)))
    parts = out_ref.shape[0]
    for tile in range(out_ref.shape[2]):
        out_ref[:, 0, tile] = result[:, tile * LANES : (tile + 1) * LANES].reshape(
            parts, out_ref.shape[3], LANES
        )


def plane_kernel(
    present_ref, in_ref, kspace_ref, sampling_ref, xf_ref, yf_ref, yi_ref, xi_ref, out_ref, misfit_ref
):
    parts, _, tiles, sub, _ = in_ref.shape
    planes = sub // 2
    rows = parts // 2 * tiles
    width_y = kspace_ref.shape[3]
    present = present_ref[0].astype(jnp.float32)
    flat_in = in_ref.reshape(parts * tiles * sub, LANES)
    flat_out = out_ref.reshape(parts * tiles * sub, LANES)
    half = LANES // 2
    low_lanes = lax.broadcasted_iota(jnp.int32, (rows, LANES), 1) < half

    def interleave(first, second):
        even = jnp.where(low_lanes, first, pltpu.roll(second, half, 1))
        odd = jnp.where(low_lanes, pltpu.roll(first, half, 1), second)
        return even, odd

    gathered = []
    for plane in range(planes):
        sides = []
        for part in range(2):
            at = 2 * plane + part
            first = flat_in[pl.ds(at, rows, stride=sub), :]
            second = flat_in[pl.ds(rows * sub + at, rows, stride=sub), :]
            sides.append(jnp.concatenate(interleave(first, second), axis=0))
        gathered.append(jnp.concatenate(sides, axis=1))
    after_x = dot(split_data(jnp.concatenate(gathered, axis=0), 1), xf_ref[...], ((1,), (0,)))
    total = jnp.zeros((8, LANES), jnp.float32)
    back = []
    for plane in range(planes):
        data = after_x[plane * width_y : (plane + 1) * width_y]
        both = dot(yf_ref[...], split_data(data, 0), ((1,), (0,)))
        spectrum_re = both[:width_y, :LANES] + both[width_y:, LANES:]
        spectrum_im = both[:width_y, LANES:] - both[width_y:, :LANES]
        weight = sampling_ref[plane].astype(jnp.float32) * present
        residual_re = weight * (spectrum_re - kspace_ref[0, 0, plane].astype(jnp.float32))
        residual_im = weight * (spectrum_im - kspace_ref[0, 1, plane].astype(jnp.float32))
        square = residual_re * residual_re + residual_im * residual_im
        total = total + jnp.sum(square.reshape(width_y // 8, 8, LANES), axis=0)
        residual = jnp.concatenate([residual_re, residual_im], axis=1)
        both = dot(yi_ref[...], split_data(residual, 0), ((1,), (0,)))
        back_re = both[:width_y, :LANES] - both[width_y:, LANES:]
        back_im = both[:width_y, LANES:] + both[width_y:, :LANES]
        back.append(jnp.concatenate([back_re, back_im], axis=1))
    returned = dot(split_data(jnp.concatenate(back, axis=0), 1), xi_ref[...], ((1,), (0,)))
    for plane in range(planes):
        for part in range(2):
            at = 2 * plane + part
            block = returned[
                plane * width_y : (plane + 1) * width_y, part * LANES : (part + 1) * LANES
            ]
            first, second = interleave(block[:rows], block[rows:])
            flat_out[pl.ds(at, rows, stride=sub), :] = first
            flat_out[pl.ds(rows * sub + at, rows, stride=sub), :] = second

    @pl.when(pl.program_id(0) == 0)
    def _():
        misfit_ref[...] = total

    @pl.when(pl.program_id(0) > 0)
    def _():
        misfit_ref[...] += total


def z_inverse_kernel(
    present_ref, in_ref, maps_ref, image_ref, table_ref, moved_ref, energy_a_ref, energy_b_ref
):
    parts, coils, _, sub, _ = in_ref.shape
    depth = image_ref.shape[3]
    present = present_ref[0].astype(jnp.float32)
    grad_re = jnp.zeros((LANES, depth), jnp.float32)
    grad_im = jnp.zeros((LANES, depth), jnp.float32)
    for coil in range(coils):
        data = in_ref[:, coil, 0].reshape(parts * sub, LANES)
        result = dot(split_data(data, 0), table_ref[...], ((0,), (0,)))
        back_re = result[:, :depth]
        back_im = result[:, depth:]
        maps_re = maps_ref[coil, 0].reshape(LANES, depth).astype(jnp.float32)
        maps_im = maps_ref[coil, 1].reshape(LANES, depth).astype(jnp.float32)
        grad_re = grad_re + (maps_re * back_re + maps_im * back_im)
        grad_im = grad_im + (maps_re * back_im - maps_im * back_re)
    shape = image_ref.shape[1:]
    moved_re = image_ref[0] - step_size * grad_re.reshape(shape)
    moved_im = image_ref[1] - step_size * grad_im.reshape(shape)
    moved_ref[0] = moved_re
    moved_ref[1] = moved_im
    energy = present * (moved_re * moved_re + moved_im * moved_im)
    cut = shape[1] // 2
    energy_a_ref[...] = energy[:, :cut]
    energy_b_ref[...] = energy[:, cut:]


def whole(array):
    zeros = (0,) * array.ndim
    return pl.BlockSpec(array.shape, lambda *_: zeros)


def params():
    return pltpu.CompilerParams(
        dimension_semantics=("arbitrary",), vmem_limit_bytes=VMEM_LIMIT
    )


def butterfly(value, axis):
    size = lax.axis_size(axis)
    span = 1
    while span < size:
        value = value + lax.ppermute(value, axis, [(i, i ^ span) for i in range(size)])
        span *= 2
    return value


def per_device(image, coil_maps, kspace, sampling, available):
    pa = lax.axis_size("pa")
    pb = lax.axis_size("pb")
    pixels = jnp.transpose(image[0], (0, 2, 1, 3))
    maps = jnp.transpose(coil_maps, (0, 1, 3, 2, 4))
    samples = kspace[0]
    mask = sampling[0]
    _, y_rows, x_rows, depth = pixels.shape
    coils = maps.shape[0]
    parts = pa * pb
    sub = 2 * depth // parts
    tiles = y_rows * x_rows // LANES
    width_x = x_rows * pa
    width_y = y_rows * pb
    order = y_order(pb, y_rows)
    zf = jnp.asarray(z_forward_table(depth))
    zi = jnp.asarray(z_inverse_table(depth))
    xf = jnp.asarray(x_table(width_x, -1.0))
    xi = jnp.asarray(x_table(width_x, 1.0))
    yf = jnp.asarray(y_forward_table(width_y, order))
    yi = jnp.asarray(y_inverse_table(width_y, order))
    buffer = jax.ShapeDtypeStruct((parts, coils, tiles, sub, LANES), jnp.float32)
    coil_block = pl.BlockSpec((parts, 1, tiles, sub, LANES), lambda j: (0, j, 0, 0, 0))
    scalar = pl.BlockSpec(memory_space=pltpu.SMEM)

    forward = pl.pallas_call(
        z_forward_kernel,
        grid=(coils,),
        out_shape=buffer,
        in_specs=[
            whole(pixels),
            pl.BlockSpec((1, 2, y_rows, x_rows, depth), lambda j: (j, 0, 0, 0, 0)),
            whole(zf),
        ],
        out_specs=coil_block,
        compiler_params=params(),
    )(pixels, maps, zf)
    received = lax.all_to_all(forward, ("pa", "pb"), split_axis=0, concat_axis=0, tiled=True)
    residual, misfit_tile = pl.pallas_call(
        plane_kernel,
        grid=(coils,),
        out_shape=(buffer, jax.ShapeDtypeStruct((8, LANES), jnp.float32)),
        in_specs=[
            scalar,
            coil_block,
            pl.BlockSpec((1,) + samples.shape[1:], lambda j: (j, 0, 0, 0, 0)),
            whole(mask),
            whole(xf),
            whole(yf),
            whole(yi),
            whole(xi),
        ],
        out_specs=(coil_block, pl.BlockSpec((8, LANES), lambda j: (0, 0))),
        compiler_params=params(),
    )(available, received, samples, mask, xf, yf, yi, xi)
    returned = lax.all_to_all(residual, ("pa", "pb"), split_axis=0, concat_axis=0, tiled=True)
    for axis in ("pb", "pa", "contrast"):
        misfit_tile = butterfly(misfit_tile, axis)
    misfit_sum = jnp.sum(misfit_tile)

    pair = LANES // x_rows
    half_energy = jax.ShapeDtypeStruct((y_rows, x_rows // 2, depth), jnp.float32)
    half_block = pl.BlockSpec((pair, x_rows // 2, depth), lambda t: (t, 0, 0))
    image_block = pl.BlockSpec((2, pair, x_rows, depth), lambda t: (0, t, 0, 0))
    moved, energy_a, energy_b = pl.pallas_call(
        z_inverse_kernel,
        grid=(tiles,),
        out_shape=(jax.ShapeDtypeStruct(pixels.shape, jnp.float32), half_energy, half_energy),
        in_specs=[
            scalar,
            pl.BlockSpec((parts, coils, 1, sub, LANES), lambda t: (0, 0, t, 0, 0)),
            pl.BlockSpec((coils, 2, pair, x_rows, depth), lambda t: (0, 0, t, 0, 0)),
            image_block,
            whole(zi),
        ],
        out_specs=(image_block, half_block, half_block),
        compiler_params=params(),
    )(available, returned, maps, pixels, zi)

    def swap(value, shift):
        size = lax.axis_size("contrast")
        pairs = []
        for low in range(shift, size + shift, 2):
            first, second = low % size, (low + 1) % size
            pairs += [(first, second), (second, first)]
        return value + lax.ppermute(value, "contrast", pairs)

    energy_a, energy_b = swap(energy_a, 0), swap(energy_b, 1)
    energy_a, energy_b = swap(energy_a, 1), swap(energy_b, 0)
    norm_value = jnp.sqrt(jnp.concatenate([energy_a, energy_b], axis=1))
    present = available[0].astype(jnp.float32)
    factor = jnp.maximum(norm_value - threshold, 0.0) / jnp.maximum(norm_value, threshold)
    shrink = present * factor
    result = jnp.transpose(moved * shrink[None], (0, 2, 1, 3))[None]
    count_all = (
        lax.axis_size("contrast") * image.shape[0] * coils * width_x * width_y * depth
    )
    return (result, misfit_sum / (2.0 * count_all))


def solution(mesh):
    return jax.shard_map(
        per_device,
        mesh=mesh,
        in_specs=(
            P("contrast", None, "pa", "pb", None),
            P(None, None, "pa", "pb", None),
            P("contrast", None, None, ("pa", "pb"), None, None),
            P("contrast", ("pa", "pb"), None, None),
            P("contrast"),
        ),
        out_specs=(P("contrast", None, "pa", "pb", None), P()),
        check_vma=False,
    )
```

```python
import functools
import math

import jax
import jax.numpy as jnp
import ml_dtypes
import numpy as np
from jax import lax
from jax.experimental import pallas as pl
from jax.experimental.pallas import tpu as pltpu
from jax.sharding import PartitionSpec as P

step_size = 1.0
threshold = 2.5
LANES = 128
VMEM_LIMIT = 40 * 1024 * 1024


def trig(length):
    index = np.arange(length)
    angles = (index[:, None] * index[None, :] % length) * (2.0 * math.pi / length)
    scale = 1.0 / math.sqrt(length)
    return np.cos(angles) * scale, np.sin(angles) * scale


def halves(table):
    high = table.astype(np.float32).astype(ml_dtypes.bfloat16)
    low = (table - high.astype(np.float64)).astype(np.float32).astype(ml_dtypes.bfloat16)
    return high, low


def left_table(table):
    high, low = halves(table)
    return np.concatenate([high, high, low], axis=1)


def right_table(table):
    high, low = halves(table)
    return np.concatenate([high, high, low], axis=0)


def split_data(value, axis):
    high = value.astype(jnp.bfloat16)
    low = (value - high.astype(jnp.float32)).astype(jnp.bfloat16)
    return jnp.concatenate([high, low, high], axis=axis)


def dot(left, right, dims):
    return lax.dot_general(left, right, (dims, ((), ())), preferred_element_type=jnp.float32)


def z_forward_table(depth):
    c, s = trig(depth)
    re_row = np.concatenate([c, s], axis=1)
    im_row = np.concatenate([-s, c], axis=1)
    return left_table(np.stack([re_row, im_row], axis=1).reshape(2 * depth, 2 * depth))


def z_inverse_table(depth):
    c, s = trig(depth)
    re_row = np.concatenate([c, s], axis=1)
    im_row = np.concatenate([-s, c], axis=1)
    return right_table(np.stack([re_row, im_row], axis=1).reshape(2 * depth, 2 * depth))


def x_table(width, sign):
    c, s = trig(width)
    s = sign * s
    return right_table(np.concatenate([np.concatenate([c, s], 1), np.concatenate([-s, c], 1)], 0))


def y_order(groups, rows):
    y = np.arange(groups * rows).reshape(groups, rows // 2, 2)
    return y.transpose(2, 0, 1).reshape(-1)


def y_forward_table(width, order):
    c, s = trig(width)
    return left_table(np.concatenate([c[:, order], s[:, order]], axis=0))


def y_inverse_table(width, order):
    c, s = trig(width)
    return left_table(np.concatenate([c[order], s[order]], axis=0))


def z_forward_kernel(image_ref, maps_ref, table_ref, out_ref):
    rows = image_ref.shape[1] * image_ref.shape[2]
    depth = image_ref.shape[3]
    image_re = image_ref[0].reshape(rows, depth)
    image_im = image_ref[1].reshape(rows, depth)
    maps_re = maps_ref[0, 0].reshape(rows, depth).astype(jnp.float32)
    maps_im = maps_ref[0, 1].reshape(rows, depth).astype(jnp.float32)
    product = jnp.concatenate(
        [maps_re * image_re - maps_im * image_im, maps_re * image_im + maps_im * image_re], axis=1
    )
    result = dot(table_ref[...], split_data(product, 1), ((1,), (1,)))
    parts = out_ref.shape[0]
    for tile in range(out_ref.shape[2]):
        out_ref[:, 0, tile] = result[:, tile * LANES : (tile + 1) * LANES].reshape(
            parts, out_ref.shape[3], LANES
        )


def plane_kernel(
    present_ref, in_ref, xf_ref, xi_ref, kspace_hbm, sampling_hbm, yf_hbm, yi_hbm, out_hbm,
    kspace_ref, sampling_ref, yf_ref, yi_ref, result_ref, misfit_ref, in_sems, out_sems, last_sem,
):
    parts, _, tiles, sub, _ = in_ref.shape
    planes = sub // 2
    rows = parts // 2 * tiles
    width_y = kspace_ref.shape[3]
    coil = pl.program_id(0)
    coils = pl.num_programs(0)
    slot = lax.rem(coil, 2)
    present = present_ref[0].astype(jnp.float32)
    half = LANES // 2
    low_lanes = lax.broadcasted_iota(jnp.int32, (rows, LANES), 1) < half
    fetches = [
        pltpu.make_async_copy(source, target, in_sems.at[n])
        for n, (source, target) in enumerate(
            [
                (yf_hbm, yf_ref),
                (sampling_hbm, sampling_ref),
                (kspace_hbm, kspace_ref),
                (yi_hbm, yi_ref),
            ]
        )
    ]

    @pl.when(coil == 0)
    def _():
        for fetch in fetches:
            fetch.start()

    def send(at, number):
        return pltpu.make_async_copy(
            result_ref.at[at], out_hbm.at[:, pl.ds(number * tiles, tiles)], out_sems.at[at]
        )

    def interleave(first, second):
        even = jnp.where(low_lanes, first, pltpu.roll(second, half, 1))
        odd = jnp.where(low_lanes, pltpu.roll(first, half, 1), second)
        return even, odd

    flat_in = in_ref.reshape(parts * tiles * sub, LANES)
    gathered = []
    for plane in range(planes):
        sides = []
        for part in range(2):
            at = 2 * plane + part
            first = flat_in[pl.ds(at, rows, stride=sub), :]
            second = flat_in[pl.ds(rows * sub + at, rows, stride=sub), :]
            sides.append(jnp.concatenate(interleave(first, second), axis=0))
        gathered.append(jnp.concatenate(sides, axis=1))
    after_x = dot(split_data(jnp.concatenate(gathered, axis=0), 1), xf_ref[...], ((1,), (0,)))

    @pl.when(coil == 0)
    def _():
        for fetch in fetches:
            fetch.wait()

    total = jnp.zeros((8, LANES), jnp.float32)
    back = []
    for plane in range(planes):
        data = after_x[plane * width_y : (plane + 1) * width_y]
        both = dot(yf_ref[...], split_data(data, 0), ((1,), (0,)))
        spectrum_re = both[:width_y, :LANES] + both[width_y:, LANES:]
        spectrum_im = both[:width_y, LANES:] - both[width_y:, :LANES]
        weight = sampling_ref[plane].astype(jnp.float32) * present
        residual_re = weight * (spectrum_re - kspace_ref[coil, 0, plane].astype(jnp.float32))
        residual_im = weight * (spectrum_im - kspace_ref[coil, 1, plane].astype(jnp.float32))
        square = residual_re * residual_re + residual_im * residual_im
        total = total + jnp.sum(square.reshape(width_y // 8, 8, LANES), axis=0)
        residual = jnp.concatenate([residual_re, residual_im], axis=1)
        both = dot(yi_ref[...], split_data(residual, 0), ((1,), (0,)))
        back_re = both[:width_y, :LANES] - both[width_y:, LANES:]
        back_im = both[:width_y, LANES:] + both[width_y:, :LANES]
        back.append(jnp.concatenate([back_re, back_im], axis=1))
    returned = dot(split_data(jnp.concatenate(back, axis=0), 1), xi_ref[...], ((1,), (0,)))

    @pl.when(coil == 0)
    def _():
        misfit_ref[0, 0] = total

    @pl.when(coil > 0)
    def _():
        misfit_ref[0, 0] += total

    @pl.when(coil > 1)
    def _():
        send(slot, coil - 2).wait()

    flat_out = result_ref.at[slot].reshape(parts * tiles * sub, LANES)
    for plane in range(planes):
        for part in range(2):
            at = 2 * plane + part
            block = returned[
                plane * width_y : (plane + 1) * width_y, part * LANES : (part + 1) * LANES
            ]
            first, second = interleave(block[:rows], block[rows:])
            flat_out[pl.ds(at, rows, stride=sub), :] = first
            flat_out[pl.ds(rows * sub + at, rows, stride=sub), :] = second
    send(slot, coil).start()

    @pl.when(coil == coils - 1)
    def _():
        misfit_ref[...] = jnp.broadcast_to(misfit_ref[0, 0][None, None], misfit_ref.shape)
        last = pltpu.make_async_copy(
            misfit_ref, out_hbm.at[:, pl.ds(coils * tiles, 1)], last_sem
        )
        last.start()
        send(1 - slot, coil - 1).wait()
        send(slot, coil).wait()
        last.wait()


def z_inverse_kernel(scale, coils, present_ref, *refs):
    data_refs = refs[:coils]
    misfit_ref, maps_ref, image_ref, table_ref, moved_ref, energy_ref = refs[coils:]
    parts, _, sub, _ = misfit_ref.shape
    depth = image_ref.shape[3]
    step = pl.program_id(0)
    present = present_ref[0].astype(jnp.float32)
    grad_re = jnp.zeros((LANES, depth), jnp.float32)
    grad_im = jnp.zeros((LANES, depth), jnp.float32)
    for coil in range(coils):
        data = data_refs[coil][:, 0].reshape(parts * sub, LANES)
        result = dot(split_data(data, 0), table_ref[...], ((0,), (0,)))
        back_re = result[:, :depth]
        back_im = result[:, depth:]
        maps_re = maps_ref[coil, 0].reshape(LANES, depth).astype(jnp.float32)
        maps_im = maps_ref[coil, 1].reshape(LANES, depth).astype(jnp.float32)
        grad_re = grad_re + (maps_re * back_re + maps_im * back_im)
        grad_im = grad_im + (maps_re * back_im - maps_im * back_re)
    shape = image_ref.shape[1:]
    moved_re = image_ref[0] - step_size * grad_re.reshape(shape)
    moved_im = image_ref[1] - step_size * grad_im.reshape(shape)
    moved_ref[0] = moved_re
    moved_ref[1] = moved_im
    energy = present * (moved_re * moved_re + moved_im * moved_im)
    count = LANES // 8
    energy_ref[pl.ds(step * count, count)] = energy.reshape(count, 8, depth)

    @pl.when(step == 0)
    def _():
        misfit = jnp.sum(misfit_ref[:, 0], axis=0)
        energy_ref[energy_ref.shape[0] - 1] = jnp.full((8, depth), jnp.sum(misfit) * scale)


def whole(array):
    zeros = (0,) * array.ndim
    return pl.BlockSpec(array.shape, lambda *_: zeros)


def params():
    return pltpu.CompilerParams(
        dimension_semantics=("arbitrary",), vmem_limit_bytes=VMEM_LIMIT
    )


def in_hbm(array):
    return pltpu.with_memory_space_constraint(array, pltpu.HBM)


def per_device(image, coil_maps, kspace, sampling, available):
    pa = lax.axis_size("pa")
    pb = lax.axis_size("pb")
    pixels = jnp.transpose(image[0], (0, 2, 1, 3))
    maps = jnp.transpose(coil_maps, (0, 1, 3, 2, 4))
    samples = kspace[0]
    mask = sampling[0]
    _, y_rows, x_rows, depth = pixels.shape
    coils = maps.shape[0]
    parts = pa * pb
    sub = 2 * depth // parts
    tiles = y_rows * x_rows // LANES
    width_x = x_rows * pa
    width_y = y_rows * pb
    order = y_order(pb, y_rows)
    zf = jnp.asarray(z_forward_table(depth))
    zi = jnp.asarray(z_inverse_table(depth))
    xf = jnp.asarray(x_table(width_x, -1.0))
    xi = jnp.asarray(x_table(width_x, 1.0))
    yf = jnp.asarray(y_forward_table(width_y, order))
    yi = jnp.asarray(y_inverse_table(width_y, order))
    buffer = pltpu.HBM((parts, coils, tiles, sub, LANES), jnp.float32)
    coil_block = pl.BlockSpec((parts, 1, tiles, sub, LANES), lambda j: (0, j, 0, 0, 0))
    scalar = pl.BlockSpec(memory_space=pltpu.SMEM)

    forward = pl.pallas_call(
        z_forward_kernel,
        grid=(coils,),
        out_shape=buffer,
        in_specs=[
            whole(pixels),
            pl.BlockSpec((1, 2, y_rows, x_rows, depth), lambda j: (j, 0, 0, 0, 0)),
            whole(zf),
        ],
        out_specs=coil_block,
        compiler_params=params(),
    )(in_hbm(pixels), in_hbm(maps), in_hbm(zf))
    received = lax.all_to_all(forward, ("pa", "pb"), split_axis=0, concat_axis=0, tiled=True)
    anywhere = pl.BlockSpec(memory_space=pl.ANY)
    residual = pl.pallas_call(
        plane_kernel,
        grid=(coils,),
        out_shape=pltpu.HBM((parts, coils * tiles + 1, sub, LANES), jnp.float32),
        in_specs=[scalar, coil_block, whole(xf), whole(xi)] + [anywhere] * 4,
        out_specs=anywhere,
        scratch_shapes=[
            pltpu.VMEM(samples.shape, samples.dtype),
            pltpu.VMEM(mask.shape, mask.dtype),
            pltpu.VMEM(yf.shape, yf.dtype),
            pltpu.VMEM(yi.shape, yi.dtype),
            pltpu.VMEM((2, parts, tiles, sub, LANES), jnp.float32),
            pltpu.VMEM((parts, 1, sub, LANES), jnp.float32),
            pltpu.SemaphoreType.DMA((4,)),
            pltpu.SemaphoreType.DMA((2,)),
            pltpu.SemaphoreType.DMA,
        ],
        compiler_params=params(),
    )(available, received, xf, xi, in_hbm(samples), in_hbm(mask), in_hbm(yf), in_hbm(yi))
    returned = lax.all_to_all(residual, ("pa", "pb"), split_axis=0, concat_axis=0, tiled=True)

    pair = LANES // x_rows
    image_block = pl.BlockSpec((2, pair, x_rows, depth), lambda t: (0, t, 0, 0))
    contrasts = lax.axis_size("contrast") * image.shape[0]
    scale = 1.0 / (2.0 * contrasts * coils * width_x * width_y * depth)
    energy_tiles = y_rows * x_rows // 8

    def tile_block(coil):
        return pl.BlockSpec((parts, 1, sub, LANES), lambda t: (0, coil * tiles + t, 0, 0))

    moved, energy = pl.pallas_call(
        functools.partial(z_inverse_kernel, scale, coils),
        grid=(tiles,),
        out_shape=(
            jax.ShapeDtypeStruct(pixels.shape, jnp.float32),
            jax.ShapeDtypeStruct((energy_tiles + 1, 8, depth), jnp.float32),
        ),
        in_specs=[scalar]
        + [tile_block(coil) for coil in range(coils)]
        + [
            pl.BlockSpec((parts, 1, sub, LANES), lambda t: (0, coils * tiles, 0, 0)),
            pl.BlockSpec((coils, 2, pair, x_rows, depth), lambda t: (0, 0, t, 0, 0)),
            image_block,
            whole(zi),
        ],
        out_specs=(
            image_block,
            pl.BlockSpec((energy_tiles + 1, 8, depth), lambda t: (0, 0, 0)),
        ),
        compiler_params=params(),
    )(available, *[returned] * (coils + 1), maps, pixels, zi)

    size = lax.axis_size("contrast")
    for step in range(2):
        pairs = []
        for core in range(pa):
            shift = (core + step) % 2
            for low in range(shift, size + shift, 2):
                first, second = low % size * pa + core, (low + 1) % size * pa + core
                pairs += [(first, second), (second, first)]
        energy = energy + lax.ppermute(energy, ("contrast", "pa"), pairs)
    norm_value = jnp.sqrt(energy[:energy_tiles].reshape(y_rows, x_rows, depth))
    present = available[0].astype(jnp.float32)
    factor = jnp.maximum(norm_value - threshold, 0.0) / jnp.maximum(norm_value, threshold)
    shrink = present * factor
    result = jnp.transpose(moved * shrink[None], (0, 2, 1, 3))[None]
    return (result, energy[energy_tiles, 0, 0])


def solution(mesh):
    return jax.shard_map(
        per_device,
        mesh=mesh,
        in_specs=(
            P("contrast", None, "pa", "pb", None),
            P(None, None, "pa", "pb", None),
            P("contrast", None, None, ("pa", "pb"), None, None),
            P("contrast", ("pa", "pb"), None, None),
            P("contrast"),
        ),
        out_specs=(P("contrast", None, "pa", "pb", None), P()),
        check_vma=False,
    )
```

```python
import functools
import math

import jax
import jax.numpy as jnp
import ml_dtypes
import numpy as np
from jax import lax
from jax.experimental import pallas as pl
from jax.experimental.pallas import tpu as pltpu
from jax.sharding import PartitionSpec as P

step_size = 1.0
threshold = 2.5
LANES = 128
VMEM_LIMIT = 40 * 1024 * 1024


def trig(length):
    index = np.arange(length)
    angles = (index[:, None] * index[None, :] % length) * (2.0 * math.pi / length)
    scale = 1.0 / math.sqrt(length)
    return np.cos(angles) * scale, np.sin(angles) * scale


def halves(table):
    high = table.astype(np.float32).astype(ml_dtypes.bfloat16)
    low = (table - high.astype(np.float64)).astype(np.float32).astype(ml_dtypes.bfloat16)
    return high, low


def left_table(table):
    high, low = halves(table)
    return np.concatenate([high, high, low], axis=1)


def right_table(table):
    high, low = halves(table)
    return np.concatenate([high, high, low], axis=0)


def split_data(value, axis):
    high = value.astype(jnp.bfloat16)
    low = (value - high.astype(jnp.float32)).astype(jnp.bfloat16)
    return jnp.concatenate([high, low, high], axis=axis)


def dot(left, right, dims):
    return lax.dot_general(left, right, (dims, ((), ())), preferred_element_type=jnp.float32)


def z_forward_table(depth):
    c, s = trig(depth)
    re_row = np.concatenate([c, s], axis=1)
    im_row = np.concatenate([-s, c], axis=1)
    return left_table(np.stack([re_row, im_row], axis=1).reshape(2 * depth, 2 * depth))


def z_inverse_table(depth):
    c, s = trig(depth)
    re_row = np.concatenate([c, s], axis=1)
    im_row = np.concatenate([-s, c], axis=1)
    return right_table(np.stack([re_row, im_row], axis=1).reshape(2 * depth, 2 * depth))


def x_table(width, sign):
    c, s = trig(width)
    s = sign * s
    return right_table(np.concatenate([np.concatenate([c, s], 1), np.concatenate([-s, c], 1)], 0))


def y_order(groups, rows):
    y = np.arange(groups * rows).reshape(groups, rows // 2, 2)
    return y.transpose(2, 1, 0).reshape(-1)


def y_tables(width, order, parity):
    c, s = trig(width)
    half = width // 2
    y = order[parity * half : (parity + 1) * half]
    forward = np.concatenate([c[:half, y], s[:half, y]], axis=0)
    back = np.concatenate([c[y, :half], s[y, :half]], axis=0)
    return left_table(forward), left_table(back)


def z_forward_kernel(
    group, present_ref, image_hbm, maps_hbm, table_hbm, out_ref, image_ref, maps_ref, table_ref, sems
):
    coils = maps_ref.shape[0]
    rows = image_ref.shape[1] * image_ref.shape[2]
    depth = image_ref.shape[3]
    tiles = rows // LANES
    parts, _, sub, _ = out_ref.shape
    copies = [
        pltpu.make_async_copy(image_hbm, image_ref, sems.at[0]),
        pltpu.make_async_copy(table_hbm, table_ref, sems.at[1]),
    ]
    for coil in range(coils):
        copies.append(
            pltpu.make_async_copy(maps_hbm.at[coil], maps_ref.at[coil], sems.at[2 + coil])
        )
    first = [copies[0], copies[2], copies[1]] + copies[3:]
    for copy in first:
        copy.start()
    copies[0].wait()
    image_re = image_ref[0].reshape(rows, depth)
    image_im = image_ref[1].reshape(rows, depth)
    for start in range(0, coils, group):
        pieces = []
        for coil in range(start, start + group):
            copies[2 + coil].wait()
            maps_re = maps_ref[coil, 0].reshape(rows, depth).astype(jnp.float32)
            maps_im = maps_ref[coil, 1].reshape(rows, depth).astype(jnp.float32)
            product = jnp.concatenate(
                [
                    maps_re * image_re - maps_im * image_im,
                    maps_re * image_im + maps_im * image_re,
                ],
                axis=1,
            )
            pieces.append(split_data(product, 1))
        if start == 0:
            copies[1].wait()
        result = dot(table_ref[...], jnp.concatenate(pieces, axis=0), ((1,), (1,)))
        for tile in range(group * tiles):
            out_ref[:, start * tiles + tile] = result[
                :, tile * LANES : (tile + 1) * LANES
            ].reshape(parts, sub, LANES)


def plane_kernel(
    group, present_ref, in_ref, xf_ref, xi_ref, kspace_ref, sampling_ref, yfe_ref, yfo_ref, yie_ref,
    yio_ref, out_ref,
):
    parts, _, sub, _ = in_ref.shape
    coils = kspace_ref.shape[0]
    tiles = in_ref.shape[1] // coils
    planes = sub // 2
    along = parts // 2
    rows = along * tiles
    width_y = kspace_ref.shape[3]
    present = present_ref[0].astype(jnp.float32)
    half = LANES // 2
    low_lanes = lax.broadcasted_iota(jnp.int32, (rows, LANES), 1) < half
    in_stride = in_ref.shape[1] * sub
    out_stride = out_ref.shape[1] * sub
    flat_in = in_ref.reshape(parts * in_stride, LANES)
    flat_out = out_ref.reshape(parts * out_stride, LANES)

    def interleave(first, second):
        even = jnp.where(low_lanes, first, pltpu.roll(second, half, 1))
        odd = jnp.where(low_lanes, pltpu.roll(first, half, 1), second)
        return even, odd

    def gather(side, coil, at):
        base = side * along * in_stride + coil * tiles * sub + at
        return jnp.concatenate(
            [flat_in[pl.ds(base + t * sub, along, stride=in_stride), :] for t in range(tiles)], axis=0
        )

    def scatter(side, coil, at, value):
        base = side * along * out_stride + coil * tiles * sub + at
        for t in range(tiles):
            flat_out[pl.ds(base + t * sub, along, stride=out_stride), :] = value[
                t * along : (t + 1) * along
            ]

    def pick(value, plane, part):
        at = (2 * plane + part) * LANES
        return value[:, at : at + LANES]

    def forward(table_ref, data):
        both = dot(table_ref[...], split_data(data, 0), ((1,), (0,)))
        c, s = both[:rows], both[rows:]
        return [
            (pick(c, p, 0) + pick(s, p, 1), pick(c, p, 1) - pick(s, p, 0)) for p in range(planes)
        ]

    def backward(table_ref, data):
        both = dot(table_ref[...], split_data(data, 0), ((1,), (0,)))
        c, s = both[:rows], both[rows:]
        return [
            (pick(c, p, 0) - pick(s, p, 1), pick(c, p, 1) + pick(s, p, 0)) for p in range(planes)
        ]

    total = jnp.zeros((8, LANES), jnp.float32)
    for start in range(0, coils, group):
        members = range(start, start + group)
        gathered = []
        for coil in members:
            for plane in range(planes):
                sides = []
                for part in range(2):
                    at = 2 * plane + part
                    sides.append(
                        jnp.concatenate(
                            interleave(gather(0, coil, at), gather(1, coil, at)), axis=0
                        )
                    )
                gathered.append(jnp.concatenate(sides, axis=1))
        after_x = dot(split_data(jnp.concatenate(gathered, axis=0), 1), xf_ref[...], ((1,), (0,)))
        back = []
        for n, coil in enumerate(members):
            at = [(n * planes + plane) * width_y for plane in range(planes)]
            even = forward(yfe_ref, jnp.concatenate([after_x[a : a + rows] for a in at], axis=1))
            odd = forward(
                yfo_ref, jnp.concatenate([after_x[a + rows : a + width_y] for a in at], axis=1)
            )
            sums, gaps = [], []
            for plane in range(planes):
                weight = sampling_ref[plane].astype(jnp.float32) * present
                for part in range(2):
                    measured = kspace_ref[coil, part, plane].astype(jnp.float32)
                    e, o = even[plane][part], odd[plane][part]
                    low = weight[:rows] * ((e + o) - measured[:rows])
                    high = weight[rows:] * ((e - o) - measured[rows:])
                    square = low * low + high * high
                    total = total + jnp.sum(square.reshape(rows // 8, 8, LANES), axis=0)
                    sums.append(low + high)
                    gaps.append(low - high)
            even = backward(yie_ref, jnp.concatenate(sums, axis=1))
            odd = backward(yio_ref, jnp.concatenate(gaps, axis=1))
            for plane in range(planes):
                back.append(jnp.concatenate(even[plane], axis=1))
                back.append(jnp.concatenate(odd[plane], axis=1))
        returned = dot(split_data(jnp.concatenate(back, axis=0), 1), xi_ref[...], ((1,), (0,)))
        for n, coil in enumerate(members):
            for plane in range(planes):
                a = (n * planes + plane) * width_y
                for part in range(2):
                    block = returned[a : a + width_y, part * LANES : (part + 1) * LANES]
                    first, second = interleave(block[:rows], block[rows:])
                    scatter(0, coil, 2 * plane + part, first)
                    scatter(1, coil, 2 * plane + part, second)
    out_ref[:, coils * tiles] = jnp.broadcast_to(total[None], (parts, sub, LANES))


def z_inverse_kernel(
    scale, present_ref, in_ref, maps_ref, image_ref, table_ref, moved_ref, energy_ref
):
    parts, _, sub, _ = in_ref.shape
    coils = maps_ref.shape[0]
    _, y_rows, x_rows, depth = image_ref.shape
    rows = y_rows * x_rows
    tiles = rows // LANES
    present = present_ref[0].astype(jnp.float32)
    grad_re = jnp.zeros((rows, depth), jnp.float32)
    grad_im = jnp.zeros((rows, depth), jnp.float32)
    for coil in range(coils):
        data = jnp.concatenate(
            [in_ref[:, coil * tiles + t].reshape(parts * sub, LANES) for t in range(tiles)], axis=1
        )
        result = dot(split_data(data, 0), table_ref[...], ((0,), (0,)))
        back_re = result[:, :depth]
        back_im = result[:, depth:]
        maps_re = maps_ref[coil, 0].reshape(rows, depth).astype(jnp.float32)
        maps_im = maps_ref[coil, 1].reshape(rows, depth).astype(jnp.float32)
        grad_re = grad_re + (maps_re * back_re + maps_im * back_im)
        grad_im = grad_im + (maps_re * back_im - maps_im * back_re)
    shape = image_ref.shape[1:]
    moved_re = image_ref[0] - step_size * grad_re.reshape(shape)
    moved_im = image_ref[1] - step_size * grad_im.reshape(shape)
    moved_ref[0] = moved_re
    moved_ref[1] = moved_im
    energy = present * (moved_re * moved_re + moved_im * moved_im)
    energy_ref[: rows // 8] = energy.reshape(rows // 8, 8, depth)
    misfit = jnp.sum(in_ref[:, coils * tiles], axis=0)
    energy_ref[rows // 8] = jnp.full((8, depth), jnp.sum(misfit) * scale)


def params():
    return pltpu.CompilerParams(vmem_limit_bytes=VMEM_LIMIT)


def in_vmem(array):
    return pltpu.with_memory_space_constraint(array, pltpu.VMEM)


def in_hbm(array):
    return pltpu.with_memory_space_constraint(array, pltpu.HBM)


def per_device(image, coil_maps, kspace, sampling, available):
    pa = lax.axis_size("pa")
    pb = lax.axis_size("pb")
    pixels = jnp.transpose(image[0], (0, 2, 1, 3))
    maps = jnp.transpose(coil_maps, (0, 1, 3, 2, 4))
    samples = kspace[0]
    mask = sampling[0]
    _, y_rows, x_rows, depth = pixels.shape
    coils = maps.shape[0]
    parts = pa * pb
    sub = 2 * depth // parts
    tiles = y_rows * x_rows // LANES
    width_x = x_rows * pa
    width_y = y_rows * pb
    order = y_order(pb, y_rows)
    zf = jnp.asarray(z_forward_table(depth))
    zi = jnp.asarray(z_inverse_table(depth))
    xf = jnp.asarray(x_table(width_x, -1.0))
    xi = jnp.asarray(x_table(width_x, 1.0))
    (yfe, yie), (yfo, yio) = (y_tables(width_y, order, parity) for parity in range(2))
    yfe, yie, yfo, yio = (jnp.asarray(table) for table in (yfe, yie, yfo, yio))
    scalar = pl.BlockSpec(memory_space=pltpu.SMEM)
    anywhere = pl.BlockSpec(memory_space=pl.ANY)
    local = pl.BlockSpec(memory_space=pltpu.VMEM)
    forward = pl.pallas_call(
        functools.partial(z_forward_kernel, 2 if coils % 2 == 0 else 1),
        out_shape=jax.ShapeDtypeStruct((parts, coils * tiles, sub, LANES), jnp.float32),
        in_specs=[scalar, anywhere, anywhere, anywhere],
        out_specs=local,
        scratch_shapes=[
            pltpu.VMEM(pixels.shape, pixels.dtype),
            pltpu.VMEM(maps.shape, maps.dtype),
            pltpu.VMEM(zf.shape, zf.dtype),
            pltpu.SemaphoreType.DMA((2 + coils,)),
        ],
        compiler_params=params(),
    )(available, in_hbm(pixels), in_hbm(maps), in_hbm(zf))
    received = lax.all_to_all(forward, ("pa", "pb"), split_axis=0, concat_axis=0, tiled=True)
    residual = pl.pallas_call(
        functools.partial(plane_kernel, coils),
        out_shape=jax.ShapeDtypeStruct((parts, coils * tiles + 1, sub, LANES), jnp.float32),
        in_specs=[scalar] + [local] * 9,
        out_specs=local,
        compiler_params=params(),
    )(
        available, received, xf, xi, in_vmem(samples), in_vmem(mask),
        in_vmem(yfe), in_vmem(yfo), in_vmem(yie), in_vmem(yio),
    )
    returned = lax.all_to_all(residual, ("pa", "pb"), split_axis=0, concat_axis=0, tiled=True)

    contrasts = lax.axis_size("contrast") * image.shape[0]
    scale = 1.0 / (2.0 * contrasts * coils * width_x * width_y * depth)
    energy_tiles = y_rows * x_rows // 8
    moved, energy = pl.pallas_call(
        functools.partial(z_inverse_kernel, scale),
        out_shape=(
            jax.ShapeDtypeStruct(pixels.shape, jnp.float32),
            jax.ShapeDtypeStruct((energy_tiles + 1, 8, depth), jnp.float32),
        ),
        in_specs=[scalar] + [local] * 4,
        out_specs=(local, local),
        compiler_params=params(),
    )(available, returned, maps, pixels, zi)

    size = lax.axis_size("contrast")
    for step in range(2):
        pairs = []
        for core in range(pa):
            shift = (core + step) % 2
            for low in range(shift, size + shift, 2):
                first, second = low % size * pa + core, (low + 1) % size * pa + core
                pairs += [(first, second), (second, first)]
        energy = energy + lax.ppermute(energy, ("contrast", "pa"), pairs)
    norm_value = jnp.sqrt(energy[:energy_tiles].reshape(y_rows, x_rows, depth))
    present = available[0].astype(jnp.float32)
    factor = jnp.maximum(norm_value - threshold, 0.0) / jnp.maximum(norm_value, threshold)
    shrink = present * factor
    result = jnp.transpose(moved * shrink[None], (0, 2, 1, 3))[None]
    return (result, energy[energy_tiles, 0, 0])


def solution(mesh):
    return jax.shard_map(
        per_device,
        mesh=mesh,
        in_specs=(
            P("contrast", None, "pa", "pb", None),
            P(None, None, "pa", "pb", None),
            P("contrast", None, None, ("pa", "pb"), None, None),
            P("contrast", ("pa", "pb"), None, None),
            P("contrast"),
        ),
        out_specs=(P("contrast", None, "pa", "pb", None), P()),
        check_vma=False,
    )
```

```python
import functools
import math

import jax
import jax.numpy as jnp
import ml_dtypes
import numpy as np
from jax import lax
from jax.experimental import pallas as pl
from jax.experimental.pallas import tpu as pltpu
from jax.sharding import PartitionSpec as P

step_size = 1.0
threshold = 2.5
LANES = 128
CHUNKS = 2
Z_CHUNK = 2
VMEM_LIMIT = 40 * 1024 * 1024


def trig(length):
    index = np.arange(length)
    angles = (index[:, None] * index[None, :] % length) * (2.0 * math.pi / length)
    scale = 1.0 / math.sqrt(length)
    return np.cos(angles) * scale, np.sin(angles) * scale


def halves(table):
    high = table.astype(np.float32).astype(ml_dtypes.bfloat16)
    low = (table - high.astype(np.float64)).astype(np.float32).astype(ml_dtypes.bfloat16)
    return high, low


def left_table(table):
    high, low = halves(table)
    return np.concatenate([high, high, low], axis=1)


def right_table(table):
    high, low = halves(table)
    return np.concatenate([high, high, low], axis=0)


def split_data(value, axis):
    high = value.astype(jnp.bfloat16)
    low = (value - high.astype(jnp.float32)).astype(jnp.bfloat16)
    return jnp.concatenate([high, low, high], axis=axis)


def dot(left, right, dims):
    return lax.dot_general(left, right, (dims, ((), ())), preferred_element_type=jnp.float32)


def z_forward_table(depth):
    c, s = trig(depth)
    re_row = np.concatenate([c, s], axis=1)
    im_row = np.concatenate([-s, c], axis=1)
    return left_table(np.stack([re_row, im_row], axis=1).reshape(2 * depth, 2 * depth))


def z_inverse_table(depth):
    c, s = trig(depth)
    re_row = np.concatenate([c, s], axis=1)
    im_row = np.concatenate([-s, c], axis=1)
    return right_table(np.stack([re_row, im_row], axis=1).reshape(2 * depth, 2 * depth))


def x_table(width, sign):
    c, s = trig(width)
    s = sign * s
    return right_table(np.concatenate([np.concatenate([c, s], 1), np.concatenate([-s, c], 1)], 0))


def y_order(groups, rows):
    y = np.arange(groups * rows).reshape(groups, rows // 2, 2)
    return y.transpose(2, 1, 0).reshape(-1)


def y_tables(width, order, parity):
    c, s = trig(width)
    half = width // 2
    y = order[parity * half : (parity + 1) * half]
    forward = np.concatenate([c[:half, y], s[:half, y]], axis=0)
    back = np.concatenate([c[y, :half], s[y, :half]], axis=0)
    return left_table(forward), left_table(back)


def z_forward_kernel(
    chunk, present_ref, image_hbm, maps_hbm, table_hbm, out_ref, image_ref, maps_ref, table_ref, sems
):
    coils = maps_ref.shape[0]
    _, y_rows, x_rows, depth = image_ref.shape
    pair = LANES // x_rows
    parts, _, sub, _ = out_ref.shape
    tiles = y_rows // pair
    table_copy = pltpu.make_async_copy(table_hbm, table_ref, sems.at[0])
    copies = []
    for t in range(0, tiles, chunk):
        along = pl.ds(t * pair, min(chunk, tiles - t) * pair)
        n = len(copies)
        copies.append(
            [
                pltpu.make_async_copy(
                    image_hbm.at[:, along], image_ref.at[:, along], sems.at[2 * n + 1]
                ),
                pltpu.make_async_copy(
                    maps_hbm.at[:, :, along], maps_ref.at[:, :, along], sems.at[2 * n + 2]
                ),
            ]
        )
    for n, both in enumerate(copies):
        for copy in both:
            copy.start()
        if n == 0:
            table_copy.start()
    for n, both in enumerate(copies):
        for copy in both:
            copy.wait()
        members = range(n * chunk, min((n + 1) * chunk, tiles))
        along = pl.ds(members.start * pair, len(members) * pair)
        rows = len(members) * LANES
        image_re = image_ref[0, along].reshape(rows, depth)
        image_im = image_ref[1, along].reshape(rows, depth)
        pieces = []
        for coil in range(coils):
            maps_re = maps_ref[coil, 0, along].reshape(rows, depth).astype(jnp.float32)
            maps_im = maps_ref[coil, 1, along].reshape(rows, depth).astype(jnp.float32)
            product = jnp.concatenate(
                [
                    maps_re * image_re - maps_im * image_im,
                    maps_re * image_im + maps_im * image_re,
                ],
                axis=1,
            )
            pieces.append(split_data(product, 1))
        if n == 0:
            table_copy.wait()
        result = dot(table_ref[...], jnp.concatenate(pieces, axis=0), ((1,), (1,)))
        for coil in range(coils):
            for m, t in enumerate(members):
                at = coil * rows + m * LANES
                out_ref[:, coil * tiles + t] = result[:, at : at + LANES].reshape(parts, sub, LANES)


def plane_kernel(
    group, present_ref, in_ref, xf_ref, xi_ref, kspace_ref, sampling_ref, yfe_ref, yfo_ref, yie_ref,
    yio_ref, out_ref,
):
    parts, _, sub, _ = in_ref.shape
    coils = kspace_ref.shape[0]
    tiles = in_ref.shape[1] // coils
    planes = sub // 2
    along = parts // 2
    rows = along * tiles
    width_y = kspace_ref.shape[3]
    present = present_ref[0].astype(jnp.float32)
    half = LANES // 2
    low_lanes = lax.broadcasted_iota(jnp.int32, (rows, LANES), 1) < half
    in_stride = in_ref.shape[1] * sub
    out_stride = out_ref.shape[1] * sub
    flat_in = in_ref.reshape(parts * in_stride, LANES)
    flat_out = out_ref.reshape(parts * out_stride, LANES)

    def interleave(first, second):
        even = jnp.where(low_lanes, first, pltpu.roll(second, half, 1))
        odd = jnp.where(low_lanes, pltpu.roll(first, half, 1), second)
        return even, odd

    def gather(side, coil, at):
        base = side * along * in_stride + coil * tiles * sub + at
        return jnp.concatenate(
            [flat_in[pl.ds(base + t * sub, along, stride=in_stride), :] for t in range(tiles)], axis=0
        )

    def scatter(side, coil, at, value):
        base = side * along * out_stride + coil * tiles * sub + at
        for t in range(tiles):
            flat_out[pl.ds(base + t * sub, along, stride=out_stride), :] = value[
                t * along : (t + 1) * along
            ]

    def pick(value, plane, part):
        at = (2 * plane + part) * LANES
        return value[:, at : at + LANES]

    def forward(table_ref, data):
        both = dot(table_ref[...], split_data(data, 0), ((1,), (0,)))
        c, s = both[:rows], both[rows:]
        return [
            (pick(c, p, 0) + pick(s, p, 1), pick(c, p, 1) - pick(s, p, 0)) for p in range(planes)
        ]

    def backward(table_ref, data):
        both = dot(table_ref[...], split_data(data, 0), ((1,), (0,)))
        c, s = both[:rows], both[rows:]
        return [
            (pick(c, p, 0) - pick(s, p, 1), pick(c, p, 1) + pick(s, p, 0)) for p in range(planes)
        ]

    def enter(members):
        gathered = []
        for coil in members:
            for plane in range(planes):
                sides = []
                for part in range(2):
                    at = 2 * plane + part
                    sides.append(
                        jnp.concatenate(
                            interleave(gather(0, coil, at), gather(1, coil, at)), axis=0
                        )
                    )
                gathered.append(jnp.concatenate(sides, axis=1))
        return dot(split_data(jnp.concatenate(gathered, axis=0), 1), xf_ref[...], ((1,), (0,)))

    def forth(members, after_x):
        total = jnp.zeros((8, LANES), jnp.float32)
        out = []
        for n, coil in enumerate(members):
            at = [(n * planes + plane) * width_y for plane in range(planes)]
            even = forward(yfe_ref, jnp.concatenate([after_x[a : a + rows] for a in at], axis=1))
            odd = forward(
                yfo_ref, jnp.concatenate([after_x[a + rows : a + width_y] for a in at], axis=1)
            )
            sums, gaps = [], []
            for plane in range(planes):
                weight = sampling_ref[plane].astype(jnp.float32) * present
                for part in range(2):
                    measured = kspace_ref[coil, part, plane].astype(jnp.float32)
                    e, o = even[plane][part], odd[plane][part]
                    low = weight[:rows] * ((e + o) - measured[:rows])
                    high = weight[rows:] * ((e - o) - measured[rows:])
                    square = low * low + high * high
                    total = total + jnp.sum(square.reshape(rows // 8, 8, LANES), axis=0)
                    sums.append(low + high)
                    gaps.append(low - high)
            out.append((jnp.concatenate(sums, axis=1), jnp.concatenate(gaps, axis=1)))
        return out, total

    def back_y(out):
        back = []
        for sums, gaps in out:
            even = backward(yie_ref, sums)
            odd = backward(yio_ref, gaps)
            for plane in range(planes):
                back.append(jnp.concatenate(even[plane], axis=1))
                back.append(jnp.concatenate(odd[plane], axis=1))
        return back

    def leave(members, back):
        returned = dot(split_data(jnp.concatenate(back, axis=0), 1), xi_ref[...], ((1,), (0,)))
        for n, coil in enumerate(members):
            for plane in range(planes):
                a = (n * planes + plane) * width_y
                for part in range(2):
                    block = returned[a : a + width_y, part * LANES : (part + 1) * LANES]
                    first, second = interleave(block[:rows], block[rows:])
                    scatter(0, coil, 2 * plane + part, first)
                    scatter(1, coil, 2 * plane + part, second)

    total = jnp.zeros((8, LANES), jnp.float32)
    groups = [range(start, start + group) for start in range(0, coils, group)]
    steps = range(len(groups))
    held = {}
    for n in range(len(groups) + 3):
        if n in steps:
            held[0, n] = enter(groups[n])
        if n - 1 in steps:
            held[1, n - 1], part_total = forth(groups[n - 1], held[0, n - 1])
            total = total + part_total
        if n - 2 in steps:
            held[2, n - 2] = back_y(held[1, n - 2])
        if n - 3 in steps:
            leave(groups[n - 3], held[2, n - 3])
    out_ref[:, coils * tiles] = jnp.broadcast_to(total[None], (parts, sub, LANES))


def z_inverse_kernel(
    scale, present_ref, in_ref, maps_ref, image_ref, table_ref, moved_ref, energy_ref
):
    parts, _, sub, _ = in_ref.shape
    coils = maps_ref.shape[0]
    _, y_rows, x_rows, depth = image_ref.shape
    rows = y_rows * x_rows
    tiles = rows // LANES
    grad_re = jnp.zeros((rows, depth), jnp.float32)
    grad_im = jnp.zeros((rows, depth), jnp.float32)
    for coil in range(coils):
        data = jnp.concatenate(
            [in_ref[:, coil * tiles + t].reshape(parts * sub, LANES) for t in range(tiles)], axis=1
        )
        result = dot(split_data(data, 0), table_ref[...], ((0,), (0,)))
        back_re = result[:, :depth]
        back_im = result[:, depth:]
        maps_re = maps_ref[coil, 0].reshape(rows, depth).astype(jnp.float32)
        maps_im = maps_ref[coil, 1].reshape(rows, depth).astype(jnp.float32)
        grad_re = grad_re + (maps_re * back_re + maps_im * back_im)
        grad_im = grad_im + (maps_re * back_im - maps_im * back_re)
    shape = image_ref.shape[1:]
    moved_re = image_ref[0] - step_size * grad_re.reshape(shape)
    moved_im = image_ref[1] - step_size * grad_im.reshape(shape)
    present = present_ref[0].astype(jnp.float32)
    moved_ref[0] = present * moved_re
    moved_ref[1] = present * moved_im
    energy = present * (moved_re * moved_re + moved_im * moved_im)
    energy_ref[: rows // 8] = energy.reshape(rows // 8, 8, depth)
    misfit = jnp.sum(in_ref[:, coils * tiles], axis=0)
    energy_ref[rows // 8] = jnp.full((8, depth), jnp.sum(misfit) * scale)


def shrink_kernel(moved_ref, energy_ref, other_ref, image_hbm, misfit_ref, image_ref, sems):
    parts, y_rows, x_rows, depth = moved_ref.shape
    cut = y_rows // CHUNKS
    count = cut * x_rows // 8
    copies = []
    for n in range(CHUNKS):
        tiles, rows = pl.ds(n * count, count), pl.ds(n * cut, cut)
        norm_value = jnp.sqrt((energy_ref[tiles] + other_ref[tiles]).reshape(cut, x_rows, depth))
        factor = jnp.maximum(norm_value - threshold, 0.0) / jnp.maximum(norm_value, threshold)
        for part in range(parts):
            image_ref[part, rows] = moved_ref[part, rows] * factor
        copies.append(
            pltpu.make_async_copy(image_ref.at[:, rows], image_hbm.at[:, rows], sems.at[n])
        )
        copies[-1].start()
    last = energy_ref.shape[0] - 1
    misfit_ref[0, 0] = jnp.max(energy_ref[last] + other_ref[last])
    for copy in copies:
        copy.wait()


def params():
    return pltpu.CompilerParams(vmem_limit_bytes=VMEM_LIMIT)


def in_vmem(array):
    return pltpu.with_memory_space_constraint(array, pltpu.VMEM)


def in_hbm(array):
    return pltpu.with_memory_space_constraint(array, pltpu.HBM)


def per_device(image, coil_maps, kspace, sampling, available):
    pa = lax.axis_size("pa")
    pb = lax.axis_size("pb")
    pixels = jnp.transpose(image[0], (0, 2, 1, 3))
    maps = jnp.transpose(coil_maps, (0, 1, 3, 2, 4))
    samples = kspace[0]
    mask = sampling[0]
    _, y_rows, x_rows, depth = pixels.shape
    coils = maps.shape[0]
    parts = pa * pb
    sub = 2 * depth // parts
    tiles = y_rows * x_rows // LANES
    width_x = x_rows * pa
    width_y = y_rows * pb
    order = y_order(pb, y_rows)
    zf = jnp.asarray(z_forward_table(depth))
    zi = jnp.asarray(z_inverse_table(depth))
    xf = jnp.asarray(x_table(width_x, -1.0))
    xi = jnp.asarray(x_table(width_x, 1.0))
    (yfe, yie), (yfo, yio) = (y_tables(width_y, order, parity) for parity in range(2))
    yfe, yie, yfo, yio = (jnp.asarray(table) for table in (yfe, yie, yfo, yio))
    scalar = pl.BlockSpec(memory_space=pltpu.SMEM)
    anywhere = pl.BlockSpec(memory_space=pl.ANY)
    local = pl.BlockSpec(memory_space=pltpu.VMEM)
    forward = pl.pallas_call(
        functools.partial(z_forward_kernel, Z_CHUNK),
        out_shape=jax.ShapeDtypeStruct((parts, coils * tiles, sub, LANES), jnp.float32),
        in_specs=[scalar] + [anywhere] * 3,
        out_specs=local,
        scratch_shapes=[
            pltpu.VMEM(pixels.shape, pixels.dtype),
            pltpu.VMEM(maps.shape, maps.dtype),
            pltpu.VMEM(zf.shape, zf.dtype),
            pltpu.SemaphoreType.DMA((2 * pl.cdiv(tiles, Z_CHUNK) + 1,)),
        ],
        compiler_params=params(),
    )(available, in_hbm(pixels), in_hbm(maps), in_hbm(zf))
    received = lax.all_to_all(forward, ("pa", "pb"), split_axis=0, concat_axis=0, tiled=True)
    residual = pl.pallas_call(
        functools.partial(plane_kernel, 1),
        out_shape=jax.ShapeDtypeStruct((parts, coils * tiles + 1, sub, LANES), jnp.float32),
        in_specs=[scalar] + [local] * 9,
        out_specs=local,
        compiler_params=params(),
    )(
        available, received, xf, xi, in_vmem(samples), in_vmem(mask),
        in_vmem(yfe), in_vmem(yfo), in_vmem(yie), in_vmem(yio),
    )
    returned = lax.all_to_all(residual, ("pa", "pb"), split_axis=0, concat_axis=0, tiled=True)

    contrasts = lax.axis_size("contrast") * image.shape[0]
    scale = 1.0 / (2.0 * contrasts * coils * width_x * width_y * depth)
    energy_tiles = y_rows * x_rows // 8
    moved, energy = pl.pallas_call(
        functools.partial(z_inverse_kernel, scale),
        out_shape=(
            jax.ShapeDtypeStruct(pixels.shape, jnp.float32),
            jax.ShapeDtypeStruct((energy_tiles + 1, 8, depth), jnp.float32),
        ),
        in_specs=[scalar] + [local] * 4,
        out_specs=(local, local),
        compiler_params=params(),
    )(available, returned, maps, pixels, zi)

    size = lax.axis_size("contrast")
    for step in range(2):
        pairs = []
        for core in range(pa):
            shift = (core + step) % 2
            for low in range(shift, size + shift, 2):
                first, second = low % size * pa + core, (low + 1) % size * pa + core
                pairs += [(first, second), (second, first)]
        other = lax.ppermute(energy, ("contrast", "pa"), pairs)
        if step == 0:
            energy = energy + other
    result, misfit = pl.pallas_call(
        shrink_kernel,
        out_shape=(
            jax.ShapeDtypeStruct(pixels.shape, jnp.float32),
            jax.ShapeDtypeStruct((1, 1), jnp.float32),
        ),
        in_specs=[local] * 3,
        out_specs=(anywhere, scalar),
        scratch_shapes=[
            pltpu.VMEM(pixels.shape, jnp.float32),
            pltpu.SemaphoreType.DMA((CHUNKS,)),
        ],
        compiler_params=params(),
    )(moved, energy, other)
    return (jnp.transpose(result, (0, 2, 1, 3))[None], misfit[0, 0])


def solution(mesh):
    return jax.shard_map(
        per_device,
        mesh=mesh,
        in_specs=(
            P("contrast", None, "pa", "pb", None),
            P(None, None, "pa", "pb", None),
            P("contrast", None, None, ("pa", "pb"), None, None),
            P("contrast", ("pa", "pb"), None, None),
            P("contrast"),
        ),
        out_specs=(P("contrast", None, "pa", "pb", None), P()),
        check_vma=False,
    )
```

```python
import functools
import math

import jax
import jax.numpy as jnp
import ml_dtypes
import numpy as np
from jax import lax
from jax.experimental import pallas as pl
from jax.experimental.pallas import tpu as pltpu
from jax.sharding import PartitionSpec as P

step_size = 1.0
threshold = 2.5
LANES = 128
CHUNKS = 2
Z_CHUNK = 2
VMEM_LIMIT = 40 * 1024 * 1024


def trig(length):
    index = np.arange(length)
    angles = (index[:, None] * index[None, :] % length) * (2.0 * math.pi / length)
    scale = 1.0 / math.sqrt(length)
    return np.cos(angles) * scale, np.sin(angles) * scale


def halves(table):
    high = table.astype(np.float32).astype(ml_dtypes.bfloat16)
    low = (table - high.astype(np.float64)).astype(np.float32).astype(ml_dtypes.bfloat16)
    return high, low


def left_table(table):
    high, low = halves(table)
    return np.concatenate([high, high, low], axis=1)


def right_table(table):
    high, low = halves(table)
    return np.concatenate([high, high, low], axis=0)


def split_data(value, axis):
    high = value.astype(jnp.bfloat16)
    low = (value - high.astype(jnp.float32)).astype(jnp.bfloat16)
    return jnp.concatenate([high, low, high], axis=axis)


def dot(left, right, dims):
    return lax.dot_general(left, right, (dims, ((), ())), preferred_element_type=jnp.float32)


def z_forward_table(depth):
    c, s = trig(depth)
    re_row = np.concatenate([c, s], axis=1)
    im_row = np.concatenate([-s, c], axis=1)
    return left_table(np.stack([re_row, im_row], axis=1).reshape(2 * depth, 2 * depth))


def z_inverse_table(depth):
    c, s = trig(depth)
    re_row = np.concatenate([c, s], axis=1)
    im_row = np.concatenate([-s, c], axis=1)
    return right_table(np.stack([re_row, im_row], axis=1).reshape(2 * depth, 2 * depth))


def x_table(width, sign):
    c, s = trig(width)
    s = sign * s
    return right_table(np.concatenate([np.concatenate([c, s], 1), np.concatenate([-s, c], 1)], 0))


def y_order(groups, rows):
    y = np.arange(groups * rows).reshape(groups, rows // 2, 2)
    return y.transpose(2, 1, 0).reshape(-1)


def y_tables(width, order, parity):
    c, s = trig(width)
    half = width // 2
    y = order[parity * half : (parity + 1) * half]
    forward = np.concatenate([c[:half, y], s[:half, y]], axis=0)
    back = np.concatenate([c[y, :half], s[y, :half]], axis=0)
    return left_table(forward), left_table(back)


def z_forward_kernel(
    chunk, present_ref, image_hbm, maps_hbm, table_hbm, out_ref, image_ref, maps_ref, table_ref, sems
):
    coils = maps_ref.shape[0]
    _, y_rows, x_rows, depth = image_ref.shape
    pair = LANES // x_rows
    parts, _, sub, _ = out_ref.shape
    tiles = y_rows // pair
    table_copy = pltpu.make_async_copy(table_hbm, table_ref, sems.at[0])
    copies = []
    for t in range(0, tiles, chunk):
        along = pl.ds(t * pair, min(chunk, tiles - t) * pair)
        n = len(copies)
        copies.append(
            [
                pltpu.make_async_copy(
                    image_hbm.at[:, along], image_ref.at[:, along], sems.at[2 * n + 1]
                ),
                pltpu.make_async_copy(
                    maps_hbm.at[:, :, along], maps_ref.at[:, :, along], sems.at[2 * n + 2]
                ),
            ]
        )
    for n, both in enumerate(copies):
        for copy in both:
            copy.start()
        if n == 0:
            table_copy.start()
    for n, both in enumerate(copies):
        for copy in both:
            copy.wait()
        members = range(n * chunk, min((n + 1) * chunk, tiles))
        along = pl.ds(members.start * pair, len(members) * pair)
        rows = len(members) * LANES
        image_re = image_ref[0, along].reshape(rows, depth)
        image_im = image_ref[1, along].reshape(rows, depth)
        pieces = []
        for coil in range(coils):
            maps_re = maps_ref[coil, 0, along].reshape(rows, depth).astype(jnp.float32)
            maps_im = maps_ref[coil, 1, along].reshape(rows, depth).astype(jnp.float32)
            product = jnp.concatenate(
                [
                    maps_re * image_re - maps_im * image_im,
                    maps_re * image_im + maps_im * image_re,
                ],
                axis=1,
            )
            pieces.append(split_data(product, 1))
        if n == 0:
            table_copy.wait()
        result = dot(table_ref[...], jnp.concatenate(pieces, axis=0), ((1,), (1,)))
        for coil in range(coils):
            for m, t in enumerate(members):
                at = coil * rows + m * LANES
                out_ref[:, coil * tiles + t] = result[:, at : at + LANES].reshape(parts, sub, LANES)


def plane_kernel(
    group, present_ref, in_ref, xf_ref, xi_ref, kspace_ref, sampling_ref, yfe_ref, yfo_ref, yie_ref,
    yio_ref, out_ref,
):
    parts, _, sub, _ = in_ref.shape
    coils = kspace_ref.shape[0]
    tiles = in_ref.shape[1] // coils
    planes = sub // 2
    along = parts // 2
    rows = along * tiles
    width_y = kspace_ref.shape[3]
    present = present_ref[0].astype(jnp.float32)
    half = LANES // 2
    low_lanes = lax.broadcasted_iota(jnp.int32, (rows, LANES), 1) < half
    in_stride = in_ref.shape[1] * sub
    out_stride = out_ref.shape[1] * sub
    flat_in = in_ref.reshape(parts * in_stride, LANES)
    flat_out = out_ref.reshape(parts * out_stride, LANES)

    def interleave(first, second):
        even = jnp.where(low_lanes, first, pltpu.roll(second, half, 1))
        odd = jnp.where(low_lanes, pltpu.roll(first, half, 1), second)
        return even, odd

    def gather(side, coil, at):
        base = side * along * in_stride + coil * tiles * sub + at
        return jnp.concatenate(
            [flat_in[pl.ds(base + t * sub, along, stride=in_stride), :] for t in range(tiles)], axis=0
        )

    def scatter(side, coil, at, value):
        base = side * along * out_stride + coil * tiles * sub + at
        for t in range(tiles):
            flat_out[pl.ds(base + t * sub, along, stride=out_stride), :] = value[
                t * along : (t + 1) * along
            ]

    def pick(value, plane, part):
        at = (2 * plane + part) * LANES
        return value[:, at : at + LANES]

    def forward(table_ref, data):
        both = dot(table_ref[...], split_data(data, 0), ((1,), (0,)))
        c, s = both[:rows], both[rows:]
        return [
            (pick(c, p, 0) + pick(s, p, 1), pick(c, p, 1) - pick(s, p, 0)) for p in range(planes)
        ]

    def backward(table_ref, data):
        both = dot(table_ref[...], split_data(data, 0), ((1,), (0,)))
        c, s = both[:rows], both[rows:]
        return [
            (pick(c, p, 0) - pick(s, p, 1), pick(c, p, 1) + pick(s, p, 0)) for p in range(planes)
        ]

    def enter(members):
        gathered = []
        for coil in members:
            for plane in range(planes):
                sides = []
                for part in range(2):
                    at = 2 * plane + part
                    sides.append(
                        jnp.concatenate(
                            interleave(gather(0, coil, at), gather(1, coil, at)), axis=0
                        )
                    )
                gathered.append(jnp.concatenate(sides, axis=1))
        return dot(split_data(jnp.concatenate(gathered, axis=0), 1), xf_ref[...], ((1,), (0,)))

    def forth(members, after_x):
        total = jnp.zeros((8, LANES), jnp.float32)
        out = []
        for n, coil in enumerate(members):
            at = [(n * planes + plane) * width_y for plane in range(planes)]
            even = forward(yfe_ref, jnp.concatenate([after_x[a : a + rows] for a in at], axis=1))
            odd = forward(
                yfo_ref, jnp.concatenate([after_x[a + rows : a + width_y] for a in at], axis=1)
            )
            sums, gaps = [], []
            for plane in range(planes):
                weight = sampling_ref[plane].astype(jnp.float32) * present
                for part in range(2):
                    measured = kspace_ref[coil, part, plane].astype(jnp.float32)
                    e, o = even[plane][part], odd[plane][part]
                    low = weight[:rows] * ((e + o) - measured[:rows])
                    high = weight[rows:] * ((e - o) - measured[rows:])
                    square = low * low + high * high
                    total = total + jnp.sum(square.reshape(rows // 8, 8, LANES), axis=0)
                    sums.append(low + high)
                    gaps.append(low - high)
            out.append((jnp.concatenate(sums, axis=1), jnp.concatenate(gaps, axis=1)))
        return out, total

    def back_y(out):
        back = []
        for sums, gaps in out:
            even = backward(yie_ref, sums)
            odd = backward(yio_ref, gaps)
            for plane in range(planes):
                back.append(jnp.concatenate(even[plane], axis=1))
                back.append(jnp.concatenate(odd[plane], axis=1))
        return back

    def leave(members, back):
        returned = dot(split_data(jnp.concatenate(back, axis=0), 1), xi_ref[...], ((1,), (0,)))
        for n, coil in enumerate(members):
            for plane in range(planes):
                a = (n * planes + plane) * width_y
                for part in range(2):
                    block = returned[a : a + width_y, part * LANES : (part + 1) * LANES]
                    first, second = interleave(block[:rows], block[rows:])
                    scatter(0, coil, 2 * plane + part, first)
                    scatter(1, coil, 2 * plane + part, second)

    total = jnp.zeros((8, LANES), jnp.float32)
    groups = [range(start, start + group) for start in range(0, coils, group)]
    steps = range(len(groups))
    held = {}
    for n in range(len(groups) + 3):
        if n in steps:
            held[0, n] = enter(groups[n])
        if n - 1 in steps:
            held[1, n - 1], part_total = forth(groups[n - 1], held[0, n - 1])
            total = total + part_total
        if n - 2 in steps:
            held[2, n - 2] = back_y(held[1, n - 2])
        if n - 3 in steps:
            leave(groups[n - 3], held[2, n - 3])
    out_ref[:, coils * tiles] = jnp.broadcast_to(total[None], (parts, sub, LANES))


def z_inverse_kernel(
    scale, present_ref, in_ref, maps_ref, image_ref, table_ref, moved_ref, *energy_refs
):
    parts, _, sub, _ = in_ref.shape
    coils = maps_ref.shape[0]
    _, y_rows, x_rows, depth = image_ref.shape
    rows = y_rows * x_rows
    tiles = rows // LANES
    grad_re = jnp.zeros((rows, depth), jnp.float32)
    grad_im = jnp.zeros((rows, depth), jnp.float32)
    for coil in range(coils):
        data = jnp.concatenate(
            [in_ref[:, coil * tiles + t].reshape(parts * sub, LANES) for t in range(tiles)], axis=1
        )
        result = dot(split_data(data, 0), table_ref[...], ((0,), (0,)))
        back_re = result[:, :depth]
        back_im = result[:, depth:]
        maps_re = maps_ref[coil, 0].reshape(rows, depth).astype(jnp.float32)
        maps_im = maps_ref[coil, 1].reshape(rows, depth).astype(jnp.float32)
        grad_re = grad_re + (maps_re * back_re + maps_im * back_im)
        grad_im = grad_im + (maps_re * back_im - maps_im * back_re)
    shape = image_ref.shape[1:]
    moved_re = image_ref[0] - step_size * grad_re.reshape(shape)
    moved_im = image_ref[1] - step_size * grad_im.reshape(shape)
    present = present_ref[0].astype(jnp.float32)
    moved_ref[0] = present * moved_re
    moved_ref[1] = present * moved_im
    energy = present * (moved_re * moved_re + moved_im * moved_im)
    energy = energy.reshape(rows // 8, 8, depth)
    cut = rows // 8 // len(energy_refs)
    for n, energy_ref in enumerate(energy_refs):
        energy_ref[:cut] = energy[n * cut : (n + 1) * cut]
    misfit = jnp.sum(in_ref[:, coils * tiles], axis=0)
    energy_refs[0][cut] = jnp.full((8, depth), jnp.sum(misfit) * scale)


def shrink_kernel(*refs):
    moved_ref = refs[0]
    energy_refs, other_refs = refs[1 : 1 + CHUNKS], refs[1 + CHUNKS : 1 + 2 * CHUNKS]
    image_hbm, misfit_ref, image_ref, sems = refs[1 + 2 * CHUNKS :]
    parts, y_rows, x_rows, depth = moved_ref.shape
    cut = y_rows // CHUNKS
    count = cut * x_rows // 8
    copies = []
    for n in range(CHUNKS):
        rows = pl.ds(n * cut, cut)
        energy = energy_refs[n][:count] + other_refs[n][:count]
        norm_value = jnp.sqrt(energy.reshape(cut, x_rows, depth))
        factor = jnp.maximum(norm_value - threshold, 0.0) / jnp.maximum(norm_value, threshold)
        for part in range(parts):
            image_ref[part, rows] = moved_ref[part, rows] * factor
        copies.append(
            pltpu.make_async_copy(image_ref.at[:, rows], image_hbm.at[:, rows], sems.at[n])
        )
        copies[-1].start()
    misfit_ref[0, 0] = jnp.max(energy_refs[0][count] + other_refs[0][count])
    for copy in copies:
        copy.wait()


def params():
    return pltpu.CompilerParams(vmem_limit_bytes=VMEM_LIMIT)


def in_vmem(array):
    return pltpu.with_memory_space_constraint(array, pltpu.VMEM)


def in_hbm(array):
    return pltpu.with_memory_space_constraint(array, pltpu.HBM)


def per_device(image, coil_maps, kspace, sampling, available):
    pa = lax.axis_size("pa")
    pb = lax.axis_size("pb")
    pixels = jnp.transpose(image[0], (0, 2, 1, 3))
    maps = jnp.transpose(coil_maps, (0, 1, 3, 2, 4))
    samples = kspace[0]
    mask = sampling[0]
    _, y_rows, x_rows, depth = pixels.shape
    coils = maps.shape[0]
    parts = pa * pb
    sub = 2 * depth // parts
    tiles = y_rows * x_rows // LANES
    width_x = x_rows * pa
    width_y = y_rows * pb
    order = y_order(pb, y_rows)
    zf = jnp.asarray(z_forward_table(depth))
    zi = jnp.asarray(z_inverse_table(depth))
    xf = jnp.asarray(x_table(width_x, -1.0))
    xi = jnp.asarray(x_table(width_x, 1.0))
    (yfe, yie), (yfo, yio) = (y_tables(width_y, order, parity) for parity in range(2))
    yfe, yie, yfo, yio = (jnp.asarray(table) for table in (yfe, yie, yfo, yio))
    scalar = pl.BlockSpec(memory_space=pltpu.SMEM)
    anywhere = pl.BlockSpec(memory_space=pl.ANY)
    local = pl.BlockSpec(memory_space=pltpu.VMEM)
    forward = pl.pallas_call(
        functools.partial(z_forward_kernel, Z_CHUNK),
        out_shape=jax.ShapeDtypeStruct((parts, coils * tiles, sub, LANES), jnp.float32),
        in_specs=[scalar] + [anywhere] * 3,
        out_specs=local,
        scratch_shapes=[
            pltpu.VMEM(pixels.shape, pixels.dtype),
            pltpu.VMEM(maps.shape, maps.dtype),
            pltpu.VMEM(zf.shape, zf.dtype),
            pltpu.SemaphoreType.DMA((2 * pl.cdiv(tiles, Z_CHUNK) + 1,)),
        ],
        compiler_params=params(),
    )(available, in_hbm(pixels), in_hbm(maps), in_hbm(zf))
    received = lax.all_to_all(forward, ("pa", "pb"), split_axis=0, concat_axis=0, tiled=True)
    residual = pl.pallas_call(
        functools.partial(plane_kernel, 1),
        out_shape=jax.ShapeDtypeStruct((parts, coils * tiles + 1, sub, LANES), jnp.float32),
        in_specs=[scalar] + [local] * 9,
        out_specs=local,
        compiler_params=params(),
    )(
        available, received, xf, xi, in_vmem(samples), in_vmem(mask),
        in_vmem(yfe), in_vmem(yfo), in_vmem(yie), in_vmem(yio),
    )
    returned = lax.all_to_all(residual, ("pa", "pb"), split_axis=0, concat_axis=0, tiled=True)

    contrasts = lax.axis_size("contrast") * image.shape[0]
    scale = 1.0 / (2.0 * contrasts * coils * width_x * width_y * depth)
    energy_tiles = y_rows * x_rows // 8 // CHUNKS
    moved, *energies = pl.pallas_call(
        functools.partial(z_inverse_kernel, scale),
        out_shape=(
            jax.ShapeDtypeStruct(pixels.shape, jnp.float32),
            *[
                jax.ShapeDtypeStruct((energy_tiles + (n == 0), 8, depth), jnp.float32)
                for n in range(CHUNKS)
            ],
        ),
        in_specs=[scalar] + [local] * 4,
        out_specs=(local,) * (1 + CHUNKS),
        compiler_params=params(),
    )(available, returned, maps, pixels, zi)

    size = lax.axis_size("contrast")

    def other_sum(value, turn):
        pairs = []
        for core in range(pa):
            shift = (core + turn) % 2
            for low in range(shift, size + shift, 2):
                first, second = low % size * pa + core, (low + 1) % size * pa + core
                pairs += [(first, second), (second, first)]
        return lax.ppermute(value, ("contrast", "pa"), pairs)

    energies = [value + other_sum(value, n) for n, value in enumerate(energies)]
    others = [other_sum(value, n + 1) for n, value in enumerate(energies)]
    result, misfit = pl.pallas_call(
        shrink_kernel,
        out_shape=(
            jax.ShapeDtypeStruct(pixels.shape, jnp.float32),
            jax.ShapeDtypeStruct((1, 1), jnp.float32),
        ),
        in_specs=[local] * (1 + 2 * CHUNKS),
        out_specs=(anywhere, scalar),
        scratch_shapes=[
            pltpu.VMEM(pixels.shape, jnp.float32),
            pltpu.SemaphoreType.DMA((CHUNKS,)),
        ],
        compiler_params=params(),
    )(moved, *energies, *others)
    return (jnp.transpose(result, (0, 2, 1, 3))[None], misfit[0, 0])


def solution(mesh):
    return jax.shard_map(
        per_device,
        mesh=mesh,
        in_specs=(
            P("contrast", None, "pa", "pb", None),
            P(None, None, "pa", "pb", None),
            P("contrast", None, None, ("pa", "pb"), None, None),
            P("contrast", ("pa", "pb"), None, None),
            P("contrast"),
        ),
        out_specs=(P("contrast", None, "pa", "pb", None), P()),
        check_vma=False,
    )
```

```python
import functools
import math

import jax
import jax.numpy as jnp
import ml_dtypes
import numpy as np
from jax import lax
from jax.experimental import pallas as pl
from jax.experimental.pallas import tpu as pltpu
from jax.sharding import PartitionSpec as P

step_size = 1.0
threshold = 2.5
LANES = 128
CHUNKS = 2
VMEM_LIMIT = 40 * 1024 * 1024


def trig(length):
    index = np.arange(length)
    angles = (index[:, None] * index[None, :] % length) * (2.0 * math.pi / length)
    scale = 1.0 / math.sqrt(length)
    return np.cos(angles) * scale, np.sin(angles) * scale


def halves(table):
    high = table.astype(np.float32).astype(ml_dtypes.bfloat16)
    low = (table - high.astype(np.float64)).astype(np.float32).astype(ml_dtypes.bfloat16)
    return high, low


def left_table(table):
    high, low = halves(table)
    return np.concatenate([high, high, low], axis=1)


def right_table(table):
    high, low = halves(table)
    return np.concatenate([high, high, low], axis=0)


def split_data(value, axis):
    high = value.astype(jnp.bfloat16)
    low = (value - high.astype(jnp.float32)).astype(jnp.bfloat16)
    return jnp.concatenate([high, low, high], axis=axis)


def dot(left, right, dims):
    return lax.dot_general(left, right, (dims, ((), ())), preferred_element_type=jnp.float32)


def z_forward_table(depth):
    c, s = trig(depth)
    re_row = np.concatenate([c, s], axis=1)
    im_row = np.concatenate([-s, c], axis=1)
    return left_table(np.stack([re_row, im_row], axis=1).reshape(2 * depth, 2 * depth))


def z_inverse_table(depth):
    c, s = trig(depth)
    re_row = np.concatenate([c, s], axis=1)
    im_row = np.concatenate([-s, c], axis=1)
    return right_table(np.stack([re_row, im_row], axis=1).reshape(2 * depth, 2 * depth))


def x_table(width, sign):
    c, s = trig(width)
    s = sign * s
    return right_table(np.concatenate([np.concatenate([c, s], 1), np.concatenate([-s, c], 1)], 0))


def y_order(groups, rows):
    y = np.arange(groups * rows).reshape(groups, rows // 2, 2)
    return y.transpose(2, 1, 0).reshape(-1)


def y_tables(width, order, parity):
    c, s = trig(width)
    half = width // 2
    y = order[parity * half : (parity + 1) * half]
    forward = np.concatenate([c[:half, y], s[:half, y]], axis=0)
    back = np.concatenate([c[y, :half], s[y, :half]], axis=0)
    return left_table(forward), left_table(back)


def z_forward_kernel(
    first, present_ref, image_hbm, maps_hbm, table_hbm, out_ref, image_ref, maps_ref, table_ref, sems
):
    coils = maps_ref.shape[0]
    _, y_rows, x_rows, depth = image_ref.shape
    pair = LANES // x_rows
    parts, _, sub, _ = out_ref.shape
    tiles = y_rows // pair
    table_copy = pltpu.make_async_copy(table_hbm, table_ref, sems.at[0])
    copies = []
    spans = [range(0, first), range(first, tiles)]
    for span in spans:
        along = pl.ds(span.start * pair, len(span) * pair)
        n = len(copies)
        copies.append(
            [
                pltpu.make_async_copy(
                    image_hbm.at[:, along], image_ref.at[:, along], sems.at[2 * n + 1]
                ),
                pltpu.make_async_copy(
                    maps_hbm.at[:, :, along], maps_ref.at[:, :, along], sems.at[2 * n + 2]
                ),
            ]
        )
    for n, both in enumerate(copies):
        for copy in both:
            copy.start()
        if n == 0:
            table_copy.start()
    for n, both in enumerate(copies):
        for copy in both:
            copy.wait()
        members = spans[n]
        along = pl.ds(members.start * pair, len(members) * pair)
        rows = len(members) * LANES
        image_re = image_ref[0, along].reshape(rows, depth)
        image_im = image_ref[1, along].reshape(rows, depth)
        pieces = []
        for coil in range(coils):
            maps_re = maps_ref[coil, 0, along].reshape(rows, depth).astype(jnp.float32)
            maps_im = maps_ref[coil, 1, along].reshape(rows, depth).astype(jnp.float32)
            product = jnp.concatenate(
                [
                    maps_re * image_re - maps_im * image_im,
                    maps_re * image_im + maps_im * image_re,
                ],
                axis=1,
            )
            pieces.append(split_data(product, 1))
        if n == 0:
            table_copy.wait()
        result = dot(table_ref[...], jnp.concatenate(pieces, axis=0), ((1,), (1,)))
        for coil in range(coils):
            for m, t in enumerate(members):
                at = coil * rows + m * LANES
                out_ref[:, coil * tiles + t] = result[:, at : at + LANES].reshape(parts, sub, LANES)


def plane_kernel(
    group, present_ref, in_ref, xf_ref, xi_ref, kspace_ref, sampling_ref, yfe_ref, yfo_ref, yie_ref,
    yio_ref, out_ref,
):
    parts, _, sub, _ = in_ref.shape
    coils = kspace_ref.shape[0]
    tiles = in_ref.shape[1] // coils
    planes = sub // 2
    along = parts // 2
    rows = along * tiles
    width_y = kspace_ref.shape[3]
    present = present_ref[0].astype(jnp.float32)
    half = LANES // 2
    low_lanes = lax.broadcasted_iota(jnp.int32, (rows, LANES), 1) < half
    in_stride = in_ref.shape[1] * sub
    out_stride = out_ref.shape[1] * sub
    flat_in = in_ref.reshape(parts * in_stride, LANES)
    flat_out = out_ref.reshape(parts * out_stride, LANES)

    def interleave(first, second):
        even = jnp.where(low_lanes, first, pltpu.roll(second, half, 1))
        odd = jnp.where(low_lanes, pltpu.roll(first, half, 1), second)
        return even, odd

    def gather(side, coil, at):
        base = side * along * in_stride + coil * tiles * sub + at
        return jnp.concatenate(
            [flat_in[pl.ds(base + t * sub, along, stride=in_stride), :] for t in range(tiles)], axis=0
        )

    def scatter(side, coil, at, value):
        base = side * along * out_stride + coil * tiles * sub + at
        for t in range(tiles):
            flat_out[pl.ds(base + t * sub, along, stride=out_stride), :] = value[
                t * along : (t + 1) * along
            ]

    def pick(value, plane, part):
        at = (2 * plane + part) * LANES
        return value[:, at : at + LANES]

    def forward(table_ref, data):
        both = dot(table_ref[...], split_data(data, 0), ((1,), (0,)))
        c, s = both[:rows], both[rows:]
        return [
            (pick(c, p, 0) + pick(s, p, 1), pick(c, p, 1) - pick(s, p, 0)) for p in range(planes)
        ]

    def backward(table_ref, data):
        both = dot(table_ref[...], split_data(data, 0), ((1,), (0,)))
        c, s = both[:rows], both[rows:]
        return [
            (pick(c, p, 0) - pick(s, p, 1), pick(c, p, 1) + pick(s, p, 0)) for p in range(planes)
        ]

    def enter(members):
        gathered = []
        for coil in members:
            for plane in range(planes):
                sides = []
                for part in range(2):
                    at = 2 * plane + part
                    sides.append(
                        jnp.concatenate(
                            interleave(gather(0, coil, at), gather(1, coil, at)), axis=0
                        )
                    )
                gathered.append(jnp.concatenate(sides, axis=1))
        return dot(split_data(jnp.concatenate(gathered, axis=0), 1), xf_ref[...], ((1,), (0,)))

    def forth(members, after_x):
        total = jnp.zeros((8, LANES), jnp.float32)
        out = []
        for n, coil in enumerate(members):
            at = [(n * planes + plane) * width_y for plane in range(planes)]
            even = forward(yfe_ref, jnp.concatenate([after_x[a : a + rows] for a in at], axis=1))
            odd = forward(
                yfo_ref, jnp.concatenate([after_x[a + rows : a + width_y] for a in at], axis=1)
            )
            sums, gaps = [], []
            for plane in range(planes):
                weight = sampling_ref[plane].astype(jnp.float32) * present
                for part in range(2):
                    measured = kspace_ref[coil, part, plane].astype(jnp.float32)
                    e, o = even[plane][part], odd[plane][part]
                    low = weight[:rows] * ((e + o) - measured[:rows])
                    high = weight[rows:] * ((e - o) - measured[rows:])
                    square = low * low + high * high
                    total = total + jnp.sum(square.reshape(rows // 8, 8, LANES), axis=0)
                    sums.append(low + high)
                    gaps.append(low - high)
            out.append((jnp.concatenate(sums, axis=1), jnp.concatenate(gaps, axis=1)))
        return out, total

    def back_y(out):
        back = []
        for sums, gaps in out:
            even = backward(yie_ref, sums)
            odd = backward(yio_ref, gaps)
            for plane in range(planes):
                back.append(jnp.concatenate(even[plane], axis=1))
                back.append(jnp.concatenate(odd[plane], axis=1))
        return back

    def leave(members, back):
        returned = dot(split_data(jnp.concatenate(back, axis=0), 1), xi_ref[...], ((1,), (0,)))
        for n, coil in enumerate(members):
            for plane in range(planes):
                a = (n * planes + plane) * width_y
                for part in range(2):
                    block = returned[a : a + width_y, part * LANES : (part + 1) * LANES]
                    first, second = interleave(block[:rows], block[rows:])
                    scatter(0, coil, 2 * plane + part, first)
                    scatter(1, coil, 2 * plane + part, second)

    total = jnp.zeros((8, LANES), jnp.float32)
    groups = [range(start, start + group) for start in range(0, coils, group)]
    steps = range(len(groups))
    held = {}
    for n in range(len(groups) + 3):
        if n in steps:
            held[0, n] = enter(groups[n])
        if n - 1 in steps:
            held[1, n - 1], part_total = forth(groups[n - 1], held[0, n - 1])
            total = total + part_total
        if n - 2 in steps:
            held[2, n - 2] = back_y(held[1, n - 2])
        if n - 3 in steps:
            leave(groups[n - 3], held[2, n - 3])
    out_ref[:, coils * tiles] = jnp.broadcast_to(total[None], (parts, sub, LANES))


def z_inverse_kernel(
    scale, present_ref, in_ref, maps_ref, image_ref, table_ref, moved_ref, *energy_refs
):
    parts, _, sub, _ = in_ref.shape
    coils = maps_ref.shape[0]
    _, y_rows, x_rows, depth = image_ref.shape
    rows = y_rows * x_rows
    tiles = rows // LANES
    grad_re = jnp.zeros((rows, depth), jnp.float32)
    grad_im = jnp.zeros((rows, depth), jnp.float32)
    for coil in range(coils):
        data = jnp.concatenate(
            [in_ref[:, coil * tiles + t].reshape(parts * sub, LANES) for t in range(tiles)], axis=1
        )
        result = dot(split_data(data, 0), table_ref[...], ((0,), (0,)))
        back_re = result[:, :depth]
        back_im = result[:, depth:]
        maps_re = maps_ref[coil, 0].reshape(rows, depth).astype(jnp.float32)
        maps_im = maps_ref[coil, 1].reshape(rows, depth).astype(jnp.float32)
        grad_re = grad_re + (maps_re * back_re + maps_im * back_im)
        grad_im = grad_im + (maps_re * back_im - maps_im * back_re)
    shape = image_ref.shape[1:]
    moved_re = image_ref[0] - step_size * grad_re.reshape(shape)
    moved_im = image_ref[1] - step_size * grad_im.reshape(shape)
    present = present_ref[0].astype(jnp.float32)
    moved_ref[0] = present * moved_re
    moved_ref[1] = present * moved_im
    energy = present * (moved_re * moved_re + moved_im * moved_im)
    energy = energy.reshape(rows // 8, 8, depth)
    cut = rows // 8 // len(energy_refs)
    for n, energy_ref in enumerate(energy_refs):
        energy_ref[:cut] = energy[n * cut : (n + 1) * cut]
    misfit = jnp.sum(in_ref[:, coils * tiles], axis=0)
    energy_refs[0][cut] = jnp.full((8, depth), jnp.sum(misfit) * scale)


def shrink_kernel(*refs):
    moved_ref = refs[0]
    energy_refs, other_refs = refs[1 : 1 + CHUNKS], refs[1 + CHUNKS : 1 + 2 * CHUNKS]
    image_hbm, misfit_ref, image_ref, sems = refs[1 + 2 * CHUNKS :]
    parts, y_rows, x_rows, depth = moved_ref.shape
    cut = y_rows // CHUNKS
    count = cut * x_rows // 8
    copies = []
    for n in range(CHUNKS):
        rows = pl.ds(n * cut, cut)
        energy = energy_refs[n][:count] + other_refs[n][:count]
        norm_value = jnp.sqrt(energy.reshape(cut, x_rows, depth))
        factor = jnp.maximum(norm_value - threshold, 0.0) / jnp.maximum(norm_value, threshold)
        for part in range(parts):
            image_ref[part, rows] = moved_ref[part, rows] * factor
        copies.append(
            pltpu.make_async_copy(image_ref.at[:, rows], image_hbm.at[:, rows], sems.at[n])
        )
        copies[-1].start()
    misfit_ref[0, 0] = jnp.max(energy_refs[0][count] + other_refs[0][count])
    for copy in copies:
        copy.wait()


def params():
    return pltpu.CompilerParams(vmem_limit_bytes=VMEM_LIMIT)


def in_vmem(array):
    return pltpu.with_memory_space_constraint(array, pltpu.VMEM)


def in_hbm(array):
    return pltpu.with_memory_space_constraint(array, pltpu.HBM)


def per_device(image, coil_maps, kspace, sampling, available):
    pa = lax.axis_size("pa")
    pb = lax.axis_size("pb")
    pixels = jnp.transpose(image[0], (0, 2, 1, 3))
    maps = jnp.transpose(coil_maps, (0, 1, 3, 2, 4))
    samples = kspace[0]
    mask = sampling[0]
    _, y_rows, x_rows, depth = pixels.shape
    coils = maps.shape[0]
    parts = pa * pb
    sub = 2 * depth // parts
    tiles = y_rows * x_rows // LANES
    width_x = x_rows * pa
    width_y = y_rows * pb
    order = y_order(pb, y_rows)
    zf = jnp.asarray(z_forward_table(depth))
    zi = jnp.asarray(z_inverse_table(depth))
    xf = jnp.asarray(x_table(width_x, -1.0))
    xi = jnp.asarray(x_table(width_x, 1.0))
    (yfe, yie), (yfo, yio) = (y_tables(width_y, order, parity) for parity in range(2))
    yfe, yie, yfo, yio = (jnp.asarray(table) for table in (yfe, yie, yfo, yio))
    scalar = pl.BlockSpec(memory_space=pltpu.SMEM)
    anywhere = pl.BlockSpec(memory_space=pl.ANY)
    local = pl.BlockSpec(memory_space=pltpu.VMEM)
    forward = pl.pallas_call(
        functools.partial(z_forward_kernel, 1),
        out_shape=jax.ShapeDtypeStruct((parts, coils * tiles, sub, LANES), jnp.float32),
        in_specs=[scalar] + [anywhere] * 3,
        out_specs=local,
        scratch_shapes=[
            pltpu.VMEM(pixels.shape, pixels.dtype),
            pltpu.VMEM(maps.shape, maps.dtype),
            pltpu.VMEM(zf.shape, zf.dtype),
            pltpu.SemaphoreType.DMA((5,)),
        ],
        compiler_params=params(),
    )(available, in_hbm(pixels), in_hbm(maps), in_hbm(zf))
    received = lax.all_to_all(forward, ("pa", "pb"), split_axis=0, concat_axis=0, tiled=True)
    residual = pl.pallas_call(
        functools.partial(plane_kernel, 1),
        out_shape=jax.ShapeDtypeStruct((parts, coils * tiles + 1, sub, LANES), jnp.float32),
        in_specs=[scalar] + [local] * 9,
        out_specs=local,
        compiler_params=params(),
    )(
        available, received, xf, xi, in_vmem(samples), in_vmem(mask),
        in_vmem(yfe), in_vmem(yfo), in_vmem(yie), in_vmem(yio),
    )
    returned = lax.all_to_all(residual, ("pa", "pb"), split_axis=0, concat_axis=0, tiled=True)

    contrasts = lax.axis_size("contrast") * image.shape[0]
    scale = 1.0 / (2.0 * contrasts * coils * width_x * width_y * depth)
    energy_tiles = y_rows * x_rows // 8 // CHUNKS
    moved, *energies = pl.pallas_call(
        functools.partial(z_inverse_kernel, scale),
        out_shape=(
            jax.ShapeDtypeStruct(pixels.shape, jnp.float32),
            *[
                jax.ShapeDtypeStruct((energy_tiles + (n == 0), 8, depth), jnp.float32)
                for n in range(CHUNKS)
            ],
        ),
        in_specs=[scalar] + [local] * 4,
        out_specs=(local,) * (1 + CHUNKS),
        compiler_params=params(),
    )(available, returned, maps, pixels, zi)

    size = lax.axis_size("contrast")

    def other_sum(value, turn):
        pairs = []
        for core in range(pa):
            shift = (core + turn) % 2
            for low in range(shift, size + shift, 2):
                first, second = low % size * pa + core, (low + 1) % size * pa + core
                pairs += [(first, second), (second, first)]
        return lax.ppermute(value, ("contrast", "pa"), pairs)

    energies = [value + other_sum(value, n) for n, value in enumerate(energies)]
    others = [other_sum(value, n + 1) for n, value in enumerate(energies)]
    result, misfit = pl.pallas_call(
        shrink_kernel,
        out_shape=(
            jax.ShapeDtypeStruct(pixels.shape, jnp.float32),
            jax.ShapeDtypeStruct((1, 1), jnp.float32),
        ),
        in_specs=[local] * (1 + 2 * CHUNKS),
        out_specs=(anywhere, scalar),
        scratch_shapes=[
            pltpu.VMEM(pixels.shape, jnp.float32),
            pltpu.SemaphoreType.DMA((CHUNKS,)),
        ],
        compiler_params=params(),
    )(moved, *energies, *others)
    return (jnp.transpose(result, (0, 2, 1, 3))[None], misfit[0, 0])


def solution(mesh):
    return jax.shard_map(
        per_device,
        mesh=mesh,
        in_specs=(
            P("contrast", None, "pa", "pb", None),
            P(None, None, "pa", "pb", None),
            P("contrast", None, None, ("pa", "pb"), None, None),
            P("contrast", ("pa", "pb"), None, None),
            P("contrast"),
        ),
        out_specs=(P("contrast", None, "pa", "pb", None), P()),
        check_vma=False,
    )
```

```python
import functools
import math

import jax
import jax.numpy as jnp
import ml_dtypes
import numpy as np
from jax import lax
from jax.experimental import pallas as pl
from jax.experimental.pallas import tpu as pltpu
from jax.sharding import PartitionSpec as P

step_size = 1.0
threshold = 2.5
LANES = 128
VMEM_LIMIT = 40 * 1024 * 1024


def trig(length):
    index = np.arange(length)
    angles = (index[:, None] * index[None, :] % length) * (2.0 * math.pi / length)
    scale = 1.0 / math.sqrt(length)
    return np.cos(angles) * scale, np.sin(angles) * scale


def halves(table):
    high = table.astype(np.float32).astype(ml_dtypes.bfloat16)
    low = (table - high.astype(np.float64)).astype(np.float32).astype(ml_dtypes.bfloat16)
    return high, low


def left_table(table):
    high, low = halves(table)
    return np.concatenate([high, high, low], axis=1)


def right_table(table):
    high, low = halves(table)
    return np.concatenate([high, high, low], axis=0)


def split_data(value, axis):
    high = value.astype(jnp.bfloat16)
    low = (value - high.astype(jnp.float32)).astype(jnp.bfloat16)
    return jnp.concatenate([high, low, high], axis=axis)


def dot(left, right, dims):
    return lax.dot_general(left, right, (dims, ((), ())), preferred_element_type=jnp.float32)


def z_forward_table(depth):
    c, s = trig(depth)
    re_row = np.concatenate([c, s], axis=1)
    im_row = np.concatenate([-s, c], axis=1)
    return left_table(np.stack([re_row, im_row], axis=1).reshape(2 * depth, 2 * depth))


def z_inverse_table(depth):
    c, s = trig(depth)
    re_row = np.concatenate([c, s], axis=1)
    im_row = np.concatenate([-s, c], axis=1)
    return right_table(np.stack([re_row, im_row], axis=1).reshape(2 * depth, 2 * depth))


def x_table(width, sign):
    c, s = trig(width)
    s = sign * s
    return right_table(np.concatenate([np.concatenate([c, s], 1), np.concatenate([-s, c], 1)], 0))


def y_order(groups, rows):
    y = np.arange(groups * rows).reshape(groups, rows // 2, 2)
    return y.transpose(2, 1, 0).reshape(-1)


def y_tables(width, order, parity):
    c, s = trig(width)
    half = width // 2
    y = order[parity * half : (parity + 1) * half]
    forward = np.concatenate([c[:half, y], s[:half, y]], axis=0)
    back = np.concatenate([c[y, :half], s[y, :half]], axis=0)
    return left_table(forward), left_table(back)


def z_forward_kernel(
    first, present_ref, image_hbm, maps_hbm, table_hbm, out_ref, image_ref, maps_ref, table_ref, sems
):
    coils = maps_ref.shape[0]
    _, y_rows, x_rows, depth = image_ref.shape
    pair = LANES // x_rows
    parts, _, sub, _ = out_ref.shape
    tiles = y_rows // pair
    table_copy = pltpu.make_async_copy(table_hbm, table_ref, sems.at[0])
    copies = []
    spans = [range(0, first), range(first, tiles)]
    for span in spans:
        along = pl.ds(span.start * pair, len(span) * pair)
        n = len(copies)
        copies.append(
            [
                pltpu.make_async_copy(
                    image_hbm.at[:, along], image_ref.at[:, along], sems.at[2 * n + 1]
                ),
                pltpu.make_async_copy(
                    maps_hbm.at[:, :, along], maps_ref.at[:, :, along], sems.at[2 * n + 2]
                ),
            ]
        )
    for n, both in enumerate(copies):
        for copy in both:
            copy.start()
        if n == 0:
            table_copy.start()
    for n, both in enumerate(copies):
        for copy in both:
            copy.wait()
        members = spans[n]
        along = pl.ds(members.start * pair, len(members) * pair)
        rows = len(members) * LANES
        image_re = image_ref[0, along].reshape(rows, depth)
        image_im = image_ref[1, along].reshape(rows, depth)
        pieces = []
        for coil in range(coils):
            maps_re = maps_ref[coil, 0, along].reshape(rows, depth).astype(jnp.float32)
            maps_im = maps_ref[coil, 1, along].reshape(rows, depth).astype(jnp.float32)
            product = jnp.concatenate(
                [
                    maps_re * image_re - maps_im * image_im,
                    maps_re * image_im + maps_im * image_re,
                ],
                axis=1,
            )
            pieces.append(split_data(product, 1))
        if n == 0:
            table_copy.wait()
        result = dot(table_ref[...], jnp.concatenate(pieces, axis=0), ((1,), (1,)))
        for coil in range(coils):
            for m, t in enumerate(members):
                at = coil * rows + m * LANES
                out_ref[:, coil * tiles + t] = result[:, at : at + LANES].reshape(parts, sub, LANES)


def plane_kernel(
    group, present_ref, in_ref, xf_ref, xi_ref, kspace_ref, sampling_ref, yfe_ref, yfo_ref, yie_ref,
    yio_ref, out_ref,
):
    parts, _, sub, _ = in_ref.shape
    coils = kspace_ref.shape[0]
    tiles = in_ref.shape[1] // coils
    planes = sub // 2
    along = parts // 2
    rows = along * tiles
    width_y = kspace_ref.shape[3]
    present = present_ref[0].astype(jnp.float32)
    half = LANES // 2
    low_lanes = lax.broadcasted_iota(jnp.int32, (rows, LANES), 1) < half
    in_stride = in_ref.shape[1] * sub
    out_stride = out_ref.shape[1] * sub
    flat_in = in_ref.reshape(parts * in_stride, LANES)
    flat_out = out_ref.reshape(parts * out_stride, LANES)

    def interleave(first, second):
        even = jnp.where(low_lanes, first, pltpu.roll(second, half, 1))
        odd = jnp.where(low_lanes, pltpu.roll(first, half, 1), second)
        return even, odd

    def gather(side, coil, at):
        base = side * along * in_stride + coil * tiles * sub + at
        return jnp.concatenate(
            [flat_in[pl.ds(base + t * sub, along, stride=in_stride), :] for t in range(tiles)], axis=0
        )

    def scatter(side, coil, at, value):
        base = side * along * out_stride + coil * tiles * sub + at
        for t in range(tiles):
            flat_out[pl.ds(base + t * sub, along, stride=out_stride), :] = value[
                t * along : (t + 1) * along
            ]

    def pick(value, plane, part):
        at = (2 * plane + part) * LANES
        return value[:, at : at + LANES]

    def forward(table_ref, data):
        both = dot(table_ref[...], split_data(data, 0), ((1,), (0,)))
        c, s = both[:rows], both[rows:]
        return [
            (pick(c, p, 0) + pick(s, p, 1), pick(c, p, 1) - pick(s, p, 0)) for p in range(planes)
        ]

    def backward(table_ref, data):
        both = dot(table_ref[...], split_data(data, 0), ((1,), (0,)))
        c, s = both[:rows], both[rows:]
        return [
            (pick(c, p, 0) - pick(s, p, 1), pick(c, p, 1) + pick(s, p, 0)) for p in range(planes)
        ]

    def enter(members):
        gathered = []
        for coil in members:
            for plane in range(planes):
                sides = []
                for part in range(2):
                    at = 2 * plane + part
                    sides.append(
                        jnp.concatenate(
                            interleave(gather(0, coil, at), gather(1, coil, at)), axis=0
                        )
                    )
                gathered.append(jnp.concatenate(sides, axis=1))
        return dot(split_data(jnp.concatenate(gathered, axis=0), 1), xf_ref[...], ((1,), (0,)))

    def forth(members, after_x):
        total = jnp.zeros((8, LANES), jnp.float32)
        out = []
        for n, coil in enumerate(members):
            at = [(n * planes + plane) * width_y for plane in range(planes)]
            even = forward(yfe_ref, jnp.concatenate([after_x[a : a + rows] for a in at], axis=1))
            odd = forward(
                yfo_ref, jnp.concatenate([after_x[a + rows : a + width_y] for a in at], axis=1)
            )
            sums, gaps = [], []
            for plane in range(planes):
                weight = sampling_ref[plane].astype(jnp.float32) * present
                for part in range(2):
                    measured = kspace_ref[coil, part, plane].astype(jnp.float32)
                    e, o = even[plane][part], odd[plane][part]
                    low = weight[:rows] * ((e + o) - measured[:rows])
                    high = weight[rows:] * ((e - o) - measured[rows:])
                    square = low * low + high * high
                    total = total + jnp.sum(square.reshape(rows // 8, 8, LANES), axis=0)
                    sums.append(low + high)
                    gaps.append(low - high)
            out.append((jnp.concatenate(sums, axis=1), jnp.concatenate(gaps, axis=1)))
        return out, total

    def back_y(out):
        back = []
        for sums, gaps in out:
            even = backward(yie_ref, sums)
            odd = backward(yio_ref, gaps)
            for plane in range(planes):
                back.append(jnp.concatenate(even[plane], axis=1))
                back.append(jnp.concatenate(odd[plane], axis=1))
        return back

    def leave(members, back):
        returned = dot(split_data(jnp.concatenate(back, axis=0), 1), xi_ref[...], ((1,), (0,)))
        for n, coil in enumerate(members):
            for plane in range(planes):
                a = (n * planes + plane) * width_y
                for part in range(2):
                    block = returned[a : a + width_y, part * LANES : (part + 1) * LANES]
                    first, second = interleave(block[:rows], block[rows:])
                    scatter(0, coil, 2 * plane + part, first)
                    scatter(1, coil, 2 * plane + part, second)

    total = jnp.zeros((8, LANES), jnp.float32)
    groups = [range(start, start + group) for start in range(0, coils, group)]
    steps = range(len(groups))
    held = {}
    for n in range(len(groups) + 3):
        if n in steps:
            held[0, n] = enter(groups[n])
        if n - 1 in steps:
            held[1, n - 1], part_total = forth(groups[n - 1], held[0, n - 1])
            total = total + part_total
        if n - 2 in steps:
            held[2, n - 2] = back_y(held[1, n - 2])
        if n - 3 in steps:
            leave(groups[n - 3], held[2, n - 3])
    out_ref[:, coils * tiles] = jnp.broadcast_to(total[None], (parts, sub, LANES))


def z_inverse_kernel(
    scale, first, present_ref, in_ref, maps_ref, image_ref, table_ref, moved_ref, energy_ref
):
    parts, stored, sub, _ = in_ref.shape
    coils = maps_ref.shape[0]
    _, y_rows, x_rows, depth = moved_ref.shape
    rows = y_rows * x_rows
    tiles = (stored - 1) // coils
    along = pl.ds(first * LANES // x_rows, y_rows)
    present = present_ref[0].astype(jnp.float32)
    grad_re = jnp.zeros((rows, depth), jnp.float32)
    grad_im = jnp.zeros((rows, depth), jnp.float32)
    for coil in range(coils):
        data = jnp.concatenate(
            [
                in_ref[:, coil * tiles + first + t].reshape(parts * sub, LANES)
                for t in range(rows // LANES)
            ],
            axis=1,
        )
        result = dot(split_data(data, 0), table_ref[...], ((0,), (0,)))
        back_re = result[:, :depth]
        back_im = result[:, depth:]
        maps_re = maps_ref[coil, 0, along].reshape(rows, depth).astype(jnp.float32)
        maps_im = maps_ref[coil, 1, along].reshape(rows, depth).astype(jnp.float32)
        grad_re = grad_re + (maps_re * back_re + maps_im * back_im)
        grad_im = grad_im + (maps_re * back_im - maps_im * back_re)
    shape = moved_ref.shape[1:]
    moved_re = image_ref[0, along] - step_size * grad_re.reshape(shape)
    moved_im = image_ref[1, along] - step_size * grad_im.reshape(shape)
    moved_ref[0] = present * moved_re
    moved_ref[1] = present * moved_im
    energy = present * (moved_re * moved_re + moved_im * moved_im)
    energy_ref[: rows // 8] = energy.reshape(rows // 8, 8, depth)
    if first == 0:
        misfit = jnp.sum(in_ref[:, coils * tiles], axis=0)
        energy_ref[rows // 8] = jnp.full((8, depth), jnp.sum(misfit) * scale)


def shrunk(moved_ref, energy_ref, other_ref, image_ref):
    shape = moved_ref.shape[1:]
    count = shape[0] * shape[1] // 8
    norm_value = jnp.sqrt((energy_ref[:count] + other_ref[:count]).reshape(shape))
    factor = jnp.maximum(norm_value - threshold, 0.0) / jnp.maximum(norm_value, threshold)
    for part in range(2):
        image_ref[part] = moved_ref[part] * factor
    return count


def shrink_first_kernel(moved_ref, energy_ref, other_ref, image_hbm, misfit_ref, image_ref, sem):
    count = shrunk(moved_ref, energy_ref, other_ref, image_ref)
    copy = pltpu.make_async_copy(image_ref, image_hbm.at[:, pl.ds(0, moved_ref.shape[1])], sem)
    copy.start()
    misfit_ref[0, 0] = jnp.max(energy_ref[count] + other_ref[count])
    copy.wait()


def shrink_rest_kernel(moved_ref, energy_ref, other_ref, _, image_hbm, image_ref, sem):
    shrunk(moved_ref, energy_ref, other_ref, image_ref)
    rows = moved_ref.shape[1]
    copy = pltpu.make_async_copy(
        image_ref, image_hbm.at[:, pl.ds(image_hbm.shape[1] - rows, rows)], sem
    )
    copy.start()
    copy.wait()


def params():
    return pltpu.CompilerParams(vmem_limit_bytes=VMEM_LIMIT)


def in_vmem(array):
    return pltpu.with_memory_space_constraint(array, pltpu.VMEM)


def in_hbm(array):
    return pltpu.with_memory_space_constraint(array, pltpu.HBM)


def per_device(image, coil_maps, kspace, sampling, available):
    pa = lax.axis_size("pa")
    pb = lax.axis_size("pb")
    pixels = jnp.transpose(image[0], (0, 2, 1, 3))
    maps = jnp.transpose(coil_maps, (0, 1, 3, 2, 4))
    samples = kspace[0]
    mask = sampling[0]
    _, y_rows, x_rows, depth = pixels.shape
    coils = maps.shape[0]
    parts = pa * pb
    sub = 2 * depth // parts
    tiles = y_rows * x_rows // LANES
    width_x = x_rows * pa
    width_y = y_rows * pb
    order = y_order(pb, y_rows)
    zf = jnp.asarray(z_forward_table(depth))
    zi = jnp.asarray(z_inverse_table(depth))
    xf = jnp.asarray(x_table(width_x, -1.0))
    xi = jnp.asarray(x_table(width_x, 1.0))
    (yfe, yie), (yfo, yio) = (y_tables(width_y, order, parity) for parity in range(2))
    yfe, yie, yfo, yio = (jnp.asarray(table) for table in (yfe, yie, yfo, yio))
    scalar = pl.BlockSpec(memory_space=pltpu.SMEM)
    anywhere = pl.BlockSpec(memory_space=pl.ANY)
    local = pl.BlockSpec(memory_space=pltpu.VMEM)
    forward = pl.pallas_call(
        functools.partial(z_forward_kernel, 1),
        out_shape=jax.ShapeDtypeStruct((parts, coils * tiles, sub, LANES), jnp.float32),
        in_specs=[scalar] + [anywhere] * 3,
        out_specs=local,
        scratch_shapes=[
            pltpu.VMEM(pixels.shape, pixels.dtype),
            pltpu.VMEM(maps.shape, maps.dtype),
            pltpu.VMEM(zf.shape, zf.dtype),
            pltpu.SemaphoreType.DMA((5,)),
        ],
        compiler_params=params(),
    )(available, in_hbm(pixels), in_hbm(maps), in_hbm(zf))
    received = lax.all_to_all(forward, ("pa", "pb"), split_axis=0, concat_axis=0, tiled=True)
    residual = pl.pallas_call(
        functools.partial(plane_kernel, 1),
        out_shape=jax.ShapeDtypeStruct((parts, coils * tiles + 1, sub, LANES), jnp.float32),
        in_specs=[scalar] + [local] * 9,
        out_specs=local,
        compiler_params=params(),
    )(
        available, received, xf, xi, in_vmem(samples), in_vmem(mask),
        in_vmem(yfe), in_vmem(yfo), in_vmem(yie), in_vmem(yio),
    )
    returned = lax.all_to_all(residual, ("pa", "pb"), split_axis=0, concat_axis=0, tiled=True)

    contrasts = lax.axis_size("contrast") * image.shape[0]
    scale = 1.0 / (2.0 * contrasts * coils * width_x * width_y * depth)
    moved, energies = [], []
    for first, last in ((0, (tiles + 1) // 2), ((tiles + 1) // 2, tiles)):
        y_part = (last - first) * LANES // x_rows
        moved_part, energy_part = pl.pallas_call(
            functools.partial(z_inverse_kernel, scale, first),
            out_shape=(
                jax.ShapeDtypeStruct((2, y_part, x_rows, depth), jnp.float32),
                jax.ShapeDtypeStruct((y_part * x_rows // 8 + (first == 0), 8, depth), jnp.float32),
            ),
            in_specs=[scalar] + [local] * 4,
            out_specs=(local, local),
            compiler_params=params(),
        )(available, returned, maps, pixels, zi)
        moved.append(moved_part)
        energies.append(energy_part)

    size = lax.axis_size("contrast")

    def other_sum(value, turn):
        pairs = []
        for core in range(pa):
            shift = (core + turn) % 2
            for low in range(shift, size + shift, 2):
                first, second = low % size * pa + core, (low + 1) % size * pa + core
                pairs += [(first, second), (second, first)]
        return lax.ppermute(value, ("contrast", "pa"), pairs)

    energies = [value + other_sum(value, n) for n, value in enumerate(energies)]
    others = [other_sum(value, n + 1) for n, value in enumerate(energies)]
    image_type = jax.ShapeDtypeStruct(pixels.shape, jnp.float32)
    scratch = [[pltpu.VMEM(part.shape, jnp.float32), pltpu.SemaphoreType.DMA] for part in moved]
    result, misfit = pl.pallas_call(
        shrink_first_kernel,
        out_shape=(image_type, jax.ShapeDtypeStruct((1, 1), jnp.float32)),
        in_specs=[local] * 3,
        out_specs=(anywhere, scalar),
        scratch_shapes=scratch[0],
        compiler_params=params(),
    )(moved[0], energies[0], others[0])
    result = pl.pallas_call(
        shrink_rest_kernel,
        out_shape=image_type,
        in_specs=[local] * 3 + [anywhere],
        out_specs=anywhere,
        scratch_shapes=scratch[1],
        input_output_aliases={3: 0},
        compiler_params=params(),
    )(moved[1], energies[1], others[1], result)
    return (jnp.transpose(result, (0, 2, 1, 3))[None], misfit[0, 0])


def solution(mesh):
    return jax.shard_map(
        per_device,
        mesh=mesh,
        in_specs=(
            P("contrast", None, "pa", "pb", None),
            P(None, None, "pa", "pb", None),
            P("contrast", None, None, ("pa", "pb"), None, None),
            P("contrast", ("pa", "pb"), None, None),
            P("contrast"),
        ),
        out_specs=(P("contrast", None, "pa", "pb", None), P()),
        check_vma=False,
    )
```
